256 devices in a mesh: blk: 32 (over y_hi, z, core), grp: 8 (over y_lo, x).
Axes of the slice: x: 4, y: 4 (y_hi: 2, y_lo: 2; y = y_hi * 2 + y_lo), z: 8, core: 2. Of those that a mesh axis runs over, the one named last changes fastest.
Arguments:
- teacher_image: bfloat16 [1280, 8192], P('grp', 'blk'), may hold values from -10.968894 to 10.968894
- teacher_text: bfloat16 [8192, 1280], P(('blk', 'grp')), may hold values from -10.968894 to 10.968894
- student_image: bfloat16 [512, 8192], P('grp', 'blk'), may hold values from -13.792653 to 13.792653
- student_text: bfloat16 [8192, 512], P(('blk', 'grp')), may hold values from -13.792653 to 13.792653
Outputs:
- image_grad: float32 [8192, 512], P(('blk', 'grp'))
- text_grad: float32 [8192, 512], P(('blk', 'grp'))
- row_loss: float32 [8192], P(('blk', 'grp'))
- column_loss: float32 [8192], P(('blk', 'grp'))
The draws below stay inside these ranges and needn't reach their ends.
All inputs are finite; a program needn't handle non-finite values.
Results may differ from the reference program's by a relative error of at most 0.004.
Values may be sent and summed in bfloat16 or wider, within the bound.
A program may use at most 64 MiB of HBM per device.

```python
import math
import jax
import jax.numpy as jnp
from jax import lax

WT = 1280
WS = 512
PAIRS = 8192


def draw_teacher_image(key, part):
    key = jax.random.fold_in(key, 1)
    return jax.random.truncated_normal(key, -4.0, 4.0, (WT, PAIRS), jnp.float32).astype(jnp.bfloat16)


def draw_teacher_text(key, part):
    key = jax.random.fold_in(key, 2)
    return jax.random.truncated_normal(key, -4.0, 4.0, (PAIRS, WT), jnp.float32).astype(jnp.bfloat16)


def draw_student_image(key, part):
    key = jax.random.fold_in(key, 3)
    return jax.random.truncated_normal(key, -4.0, 4.0, (WS, PAIRS), jnp.float32).astype(jnp.bfloat16)


def draw_student_text(key, part):
    key = jax.random.fold_in(key, 4)
    return jax.random.truncated_normal(key, -4.0, 4.0, (PAIRS, WS), jnp.float32).astype(jnp.bfloat16)


def setup_inputs(seed: int = 0) -> dict:
    seeds = jax.random.split(jax.random.key(seed), 5)
    teacher_image = draw_teacher_image(jax.random.fold_in(seeds[4], 71), 0)
    teacher_text = draw_teacher_text(jax.random.fold_in(seeds[4], 71), 0)
    student_image = draw_student_image(jax.random.fold_in(seeds[4], 71), 0)
    student_text = draw_student_text(jax.random.fold_in(seeds[4], 71), 0)
    return dict(teacher_image=teacher_image, teacher_text=teacher_text, student_image=student_image, student_text=student_text)


def similarity(left, right, scale):
    return lax.dot_general(left, right, (((1,), (0,)), ((), ())), preferred_element_type=jnp.float32) * scale

def reference(teacher_image, teacher_text, student_image, student_text):
    scale_t = 1.0 / math.sqrt(WT)
    scale_s = 1.0 / math.sqrt(WS)
    block_size = math.gcd(PAIRS, 512)
    block_count = PAIRS // block_size
    texts_t = teacher_text.reshape(block_count, block_size, WT)
    texts_s = student_text.reshape(block_count, block_size, WS)

    def first_pass(carry, blocks):
        block_t, block_s = blocks
        logit_t = similarity(block_t, teacher_image, scale_t)
        logit_s = similarity(block_s, student_image, scale_s)
        top_t = jnp.maximum(carry[0], lax.optimization_barrier(jnp.max(logit_t, axis=0)))
        total_t = carry[1] * jnp.exp(carry[0] - top_t) + lax.optimization_barrier(jnp.sum(jnp.exp(logit_t - top_t[None, :]), axis=0))
        top_s = jnp.maximum(carry[2], lax.optimization_barrier(jnp.max(logit_s, axis=0)))
        total_s = carry[3] * jnp.exp(carry[2] - top_s) + lax.optimization_barrier(jnp.sum(jnp.exp(logit_s - top_s[None, :]), axis=0))
        columns = (jax.nn.logsumexp(logit_t, axis=1), jax.nn.logsumexp(logit_s, axis=1))
        return ((top_t, total_t, top_s, total_s), columns)
    lowest = jnp.full((PAIRS,), -1e+30, jnp.float32)
    nothing = jnp.zeros((PAIRS,), jnp.float32)
    stats, columns = lax.scan(first_pass, (lowest, nothing, lowest, nothing), (texts_t, texts_s))
    row_lse_t = stats[0] + jnp.log(stats[1])
    row_lse_s = stats[2] + jnp.log(stats[3])

    def second_pass(carry, blocks):
        block_t, block_s, col_t, col_s = blocks
        logit_t = similarity(block_t, teacher_image, scale_t)
        logit_s = similarity(block_s, student_image, scale_s)
        prob_t = jnp.exp(logit_t - row_lse_t[None, :])
        prob_s = jnp.exp(logit_s - row_lse_s[None, :])
        share_t = jnp.exp(logit_t - col_t[:, None])
        share_s = jnp.exp(logit_s - col_s[:, None])
        gap = logit_t - logit_s
        weights = (PAIRS * (prob_s - prob_t + share_s - share_t)).astype(jnp.bfloat16)
        image_acc = carry[0] + lax.dot_general(weights, block_s, (((0,), (0,)), ((), ())), preferred_element_type=jnp.float32)
        row_acc = carry[1] + lax.optimization_barrier(jnp.sum(prob_t * gap, axis=0))
        text_part = lax.dot_general(weights, student_image, (((1,), (1,)), ((), ())), preferred_element_type=jnp.float32) * scale_s
        column_part = lax.optimization_barrier(jnp.sum(share_t * gap, axis=1)) - col_t + col_s
        return ((image_acc, row_acc), (text_part, column_part))
    start = (jnp.zeros((PAIRS, WS), jnp.float32), jnp.zeros((PAIRS,), jnp.float32))
    sums, outputs = lax.scan(second_pass, start, (texts_t, texts_s, columns[0], columns[1]))
    image_grad = sums[0] * scale_s
    row_loss = sums[1] - row_lse_t + row_lse_s
    text_grad = outputs[0].reshape(PAIRS, WS)
    column_loss = outputs[1].reshape(PAIRS)
    return (image_grad, text_grad, row_loss, column_loss)
```

```python
import functools
import math

import jax
import jax.numpy as jnp
from jax import lax
from jax.experimental import pallas as pl
from jax.experimental.pallas import tpu as pltpu
from jax.sharding import PartitionSpec as P

MESH = pl.DeviceIdType.MESH
X, Y, Z = 4, 4, 8
PLANE, LINE = X * Y, 2 * Z
ROWS = 32
CHUNK = 128
F32 = jnp.float32
BF16 = jnp.bfloat16


class Place:
    def __init__(self):
        blk = lax.axis_index("blk")
        grp = lax.axis_index("grp")
        self.core = blk % 2
        self.z = (blk // 2) % Z
        self.y = (blk // LINE) * 2 + grp // X
        self.x = grp % X

    def at(self, x=None, y=None, z=None, core=None):
        x = self.x if x is None else x
        y = self.y if y is None else y
        z = self.z if z is None else z
        core = self.core if core is None else core
        return ((y // 2) * LINE + z * 2 + core, (y % 2) * X + x)

    def in_plane(self, slot):
        return self.at(x=slot % X, y=slot // X)

    def in_line(self, slot):
        return self.at(z=slot % Z, core=slot // Z)


def wait_for(ref, sem):
    pltpu.make_async_copy(ref, ref, sem).wait()


def send(src, dst, send_sem, recv_sem, device):
    pltpu.make_async_remote_copy(
        src_ref=src,
        dst_ref=dst,
        send_sem=send_sem,
        recv_sem=recv_sem,
        device_id=device,
        device_id_type=MESH,
    ).start()


class Line:
    def __init__(self, me, buf, send_sem, recv_sem, sib_sem):
        self.me, self.buf, self.ss, self.rs, self.sib = me, buf, send_sem, recv_sem, sib_sem

    def block(self, dz):
        me = self.me
        return self.buf.at[me.core * Z + (me.z + dz + Z) % Z]

    def hop(self, k):
        me = self.me
        up, down = me.at(z=(me.z + 1) % Z), me.at(z=(me.z + Z - 1) % Z)
        if k < 3:
            a, b = self.block(-k), self.block(k)
            send(a, a, self.ss, self.rs.at[2 * k], up)
            send(b, b, self.ss, self.rs.at[2 * k + 1], down)
        else:
            half = ROWS // 2
            a, b = self.block(-k).at[pl.ds(0, half)], self.block(k).at[pl.ds(half, half)]
            send(a, a, self.ss, self.rs.at[6], up)
            send(b, b, self.ss, self.rs.at[6], down)

    def share(self, dz):
        me = self.me
        ref = self.block(dz)
        send(ref, ref, self.ss, self.sib, me.at(core=1 - me.core))

    def begin(self):
        self.hop(0)
        self.share(0)

    def round(self, k):
        if k < 4:
            wait_for(self.block(-k), self.rs.at[2 * (k - 1)])
            wait_for(self.block(k), self.rs.at[2 * (k - 1) + 1])
            self.hop(k)
            self.share(-k)
            self.share(k)
        else:
            wait_for(self.block(4), self.rs.at[6])
            self.share(4)

    def finish(self):
        wait_for(self.buf.at[pl.ds((1 - self.me.core) * Z, Z)], self.sib)


class Sheet:
    def __init__(self, me, buf, first_row, rows, x_first, send_sem, recv_sem):
        self.me, self.buf, self.r0, self.n = me, buf, first_row, rows
        self.x_first, self.ss, self.rs = x_first, send_sem, recv_sem

    def block(self, d1, d2, cols=None):
        me = self.me
        dx, dy = (d1, d2) if self.x_first else (d2, d1)
        slot = ((me.y + dy + Y) % Y) * X + (me.x + dx + X) % X
        rows = pl.ds(self.r0, self.n)
        if cols is None:
            return self.buf.at[slot, rows]
        return self.buf.at[slot, rows, pl.ds(cols * 128, 128)]

    def to(self, axis, by):
        me = self.me
        if (axis == 1) == self.x_first:
            return me.at(x=(me.x + by + X) % X)
        return me.at(y=(me.y + by + Y) % Y)


    ORDER = (0, -1, 1, 2)

    def begin(self):
        ref = self.block(0, 0)
        send(ref, ref, self.ss, self.rs.at[0], self.to(1, 1))
        send(ref, ref, self.ss, self.rs.at[1], self.to(1, -1))

    def second(self, i):
        ref = self.block(self.ORDER[i], 0)
        send(ref, ref, self.ss, self.rs.at[3 + 2 * i], self.to(2, 1))
        send(ref, ref, self.ss, self.rs.at[4 + 2 * i], self.to(2, -1))

    def near(self):
        wait_for(self.block(-1, 0), self.rs.at[0])
        wait_for(self.block(1, 0), self.rs.at[1])
        a, b = self.block(-1, 0, 0), self.block(1, 0, 1)
        send(a, a, self.ss, self.rs.at[2], self.to(1, 1))
        send(b, b, self.ss, self.rs.at[2], self.to(1, -1))
        self.second(1)
        self.second(2)

    def far(self):
        wait_for(self.block(2, 0), self.rs.at[2])
        self.second(3)

    def last(self, i):
        d = self.ORDER[i]
        wait_for(self.block(d, -1), self.rs.at[3 + 2 * i])
        wait_for(self.block(d, 1), self.rs.at[4 + 2 * i])
        a, b = self.block(d, -1, 0), self.block(d, 1, 1)
        send(a, a, self.ss, self.rs.at[11], self.to(2, 1))
        send(b, b, self.ss, self.rs.at[11], self.to(2, -1))

    def finish(self):
        me = self.me
        rows = pl.ds(self.r0, self.n)
        wait_for(self.buf.at[pl.ds(0, 4), rows], self.rs.at[11])


def diagonal():
    rows = lax.broadcasted_iota(jnp.int32, (CHUNK, CHUNK), 0)
    cols = lax.broadcasted_iota(jnp.int32, (CHUNK, CHUNK), 1)
    return rows == cols


def to_lanes(column):
    return jnp.sum(jnp.where(diagonal(), column, 0.0), axis=0, keepdims=True)


def to_rows(lanes):
    return jnp.sum(jnp.where(diagonal(), lanes, 0.0), axis=1, keepdims=True)


def dot(a, b, ca, cb):
    return lax.dot_general(a, b, (((ca,), (cb,)), ((), ())), preferred_element_type=F32)


def across(parts):
    return jnp.concatenate(parts, axis=1)


def kernel(
    stage,
    ti_hbm, tt_hbm, si_hbm, st_hbm,
    image_out, text_out, row_out, col_out,
    tt, st, it, is_, t2, ert, ect, ers, ecs, w, col_max, row_max, row_sum, row_kl,
    msg_l, msg_p, kl_l, kl_p, got_l, got_p, gotk_l, gotk_p,
    tp, tsib, tc, ip, rt, ri,
    local_sem, line_s, line_r, sib_r, plane_s, plane_r,
    small_s, small_r, grad_s, grad_r,
):
    me = Place()
    images = it.shape[0] // 8 * 256
    texts = LINE * ROWS
    teacher, student = tt.shape[2], st.shape[2]
    pairs = float(PLANE * LINE * ROWS)
    mine_p = me.y * X + me.x
    mine_l = me.core * Z + me.z

    own = [
        pltpu.make_async_copy(tt_hbm, tt.at[mine_l], local_sem.at[0]),
        pltpu.make_async_copy(ti_hbm, it.at[mine_p], local_sem.at[1]),
        pltpu.make_async_copy(st_hbm, st.at[mine_l], local_sem.at[2]),
        pltpu.make_async_copy(si_hbm, is_.at[mine_p], local_sem.at[3]),
    ]
    for copy in own:
        copy.start()
    barrier = pltpu.get_barrier_semaphore()

    def greet(d, carry):
        pl.semaphore_signal(barrier, inc=1, device_id=me.in_line((mine_l + d) % LINE), device_id_type=MESH)
        pl.semaphore_signal(barrier, inc=1, device_id=me.in_plane((mine_p + d) % PLANE), device_id_type=MESH)
        return carry

    lax.fori_loop(1, 16, greet, 0)
    for copy in own:
        copy.wait()
    pl.semaphore_wait(barrier, 30)

    lines = [Line(me, buf, line_s.at[n], line_r.at[n], sib_r.at[n]) for n, buf in enumerate((tt, st))]
    sheets = []
    for n, buf in enumerate((it, is_)):
        half = buf.shape[1] // 2
        sheets.append(
            [
                Sheet(me, buf, 0, half, True, plane_s.at[n], plane_r.at[2 * n]),
                Sheet(me, buf, half, half, False, plane_s.at[n], plane_r.at[2 * n + 1]),
            ]
        )
    for n in range(2):
        lines[n].begin()
        for sheet in sheets[n]:
            sheet.begin()
        for sheet in sheets[n]:
            sheet.second(0)
    for n in range(2):
        lines[n].round(1)
        for sheet in sheets[n]:
            sheet.near()
        for sheet in sheets[n]:
            sheet.last(0)
    for n in range(2):
        lines[n].round(2)
        for sheet in sheets[n]:
            sheet.far()
        for i in (1, 2):
            for sheet in sheets[n]:
                sheet.last(i)
    for n in range(2):
        lines[n].round(3)
        for sheet in sheets[n]:
            sheet.last(3)
    for n in range(2):
        lines[n].round(4)
        for sheet in sheets[n]:
            sheet.finish()
        lines[n].finish()

    if stage >= 2:
        blocks = images // 256
        keep = 256 // ROWS
        scale_t = math.log2(math.e) / math.sqrt(teacher)
        scale_s = math.log2(math.e) / math.sqrt(student)
        cut = CHUNK // ROWS

        def logits(k, carry):
            rows = pl.ds(pl.multiple_of(k * CHUNK, CHUNK), CHUNK)
            mine = pl.ds(k * cut, cut)
            for which in range(2):
                src, img, er, ec = ((tt, it, ert, ect), (st, is_, ers, ecs))[which]
                width = src.shape[2]
                block = src[mine].reshape(CHUNK, width)
                scale = (scale_t, scale_s)[which]
                tiles = [
                    dot(block, img[pl.ds(a * keep, keep)].reshape(width, 256), 1, 0) * scale for a in range(blocks)
                ]
                top = jnp.max(functools.reduce(jnp.maximum, tiles), axis=1, keepdims=True)
                col_max[which, rows] = top
                col_parts = []
                kl_parts = []
                gaps = []
                for a in range(blocks):
                    cols = pl.ds(a * 256, 256)
                    e_col = jnp.exp2(tiles[a] - top)
                    ec[rows, cols] = e_col
                    col_parts.append(e_col)
                    high = jnp.max(tiles[a], axis=0, keepdims=True)
                    e_row = jnp.exp2(tiles[a] - high)
                    er[rows, cols] = e_row
                    row_max[which, pl.ds(k, 1), cols] = high
                    row_sum[which, pl.ds(k, 1), cols] = jnp.sum(e_row, axis=0, keepdims=True)
                    if which == 0:
                        t2[rows, cols] = tiles[a]
                    else:
                        gap = t2[rows, cols] - tiles[a]
                        kl_parts.append(ect[rows, cols] * gap)
                        row_kl[pl.ds(k, 1), cols] = jnp.sum(ert[rows, cols] * gap, axis=0, keepdims=True)
                total = jnp.sum(functools.reduce(jnp.add, col_parts), axis=1, keepdims=True)
                msg_l[pl.ds(4 * which + k, 1), :] = to_lanes(top + jnp.log2(total))
                if which == 0:
                    total_t = total
                else:
                    kl = jnp.sum(functools.reduce(jnp.add, kl_parts), axis=1, keepdims=True)
                    kl_l[pl.ds(k, 1), :] = to_lanes(kl / total_t)
            return carry

        kl_l[...] = jnp.zeros_like(kl_l)
        kl_p[...] = jnp.zeros_like(kl_p)
        lax.fori_loop(0, texts // CHUNK, logits, 0)
        for which in range(2):
            high = row_max[which]
            top = jnp.max(high, axis=0, keepdims=True)
            part = jnp.exp2(high - top)
            total = jnp.sum(row_sum[which] * part, axis=0, keepdims=True)
            lse = top + jnp.log2(total)
            for a in range(4):
                msg_p[4 * which + a : 4 * which + a + 1, :] = lse[:, a * 128 : a * 128 + 128]
            if which == 0:
                kl = jnp.sum(row_kl[...] * part, axis=0, keepdims=True) / total
                for a in range(4):
                    kl_p[a : a + 1, :] = kl[:, a * 128 : a * 128 + 128]

    if stage >= 3:
        groups = ((msg_p, kl_p, got_p, gotk_p, me.in_plane, mine_p), (msg_l, kl_l, got_l, gotk_l, me.in_line, mine_l))
        for n in range(2):

            def tell(d, carry):
                for g, (msg, kl, got, gotk, where, mine) in enumerate(groups):
                    src, dst = ((msg, got), (kl, gotk))[n]
                    send(src, dst.at[d], small_s.at[n, g], small_r.at[n, g], where((mine + d) % 16))
                return carry

            lax.fori_loop(1, 16, tell, 0)
        lse = []
        for g, (msg, kl, got, gotk, where, mine) in enumerate(groups):
            got[0] = msg[...]
            wait_for(got.at[pl.ds(1, 15)], small_r.at[0, g])
            every = got[...]
            top = jnp.max(every, axis=0)
            lse.append(top + jnp.log2(jnp.sum(jnp.exp2(every - top[None]), axis=0)))

    if stage >= 4:
        image_lse = [across([lse[0][4 * which + a : 4 * which + a + 1, :] for a in range(4)]) for which in range(2)]
        got_l[0] = lse[1]
        half_slots = Z

        def weigh(n, carry):
            k = ((1 - me.core) * 2 + n) % 4
            rows = pl.ds(pl.multiple_of(k * CHUNK, CHUNK), CHUNK)
            factors = []
            for which in range(2):
                by_row = jnp.exp2(row_max[which, pl.ds(k, 1), :] - image_lse[which]) * pairs
                col_lse = to_rows(got_l[0, pl.ds(4 * which + k, 1), :])
                by_col = jnp.exp2(col_max[which, rows] - col_lse) * pairs
                factors.append((by_row, by_col))
            (row_t, col_t), (row_s, col_s) = factors
            total = None
            for a in range(images // 256):
                cols = pl.ds(a * 256, 256)
                lanes = slice(a * 256, a * 256 + 256)
                weights = (
                    ers[rows, cols] * row_s[:, lanes]
                    - ert[rows, cols] * row_t[:, lanes]
                    + ecs[rows, cols] * col_s
                    - ect[rows, cols] * col_t
                ).astype(BF16)
                w[rows, cols] = weights
                part = dot(weights, is_[pl.ds(a * 8, 8)].reshape(student, 256), 1, 1)
                total = part if total is None else total + part
            tp[pl.ds(k * 4, 4)] = total.astype(BF16).reshape(4, ROWS, student)
            return carry

        other = pl.ds((1 - me.core) * Z, Z)
        lax.fori_loop(0, 2, weigh, 0)
        send(tp.at[other], tsib, grad_s.at[0], grad_r.at[0], me.at(core=1 - me.core))
        lax.fori_loop(2, 4, weigh, 0)

        texts_s = st[...].reshape(texts, student)
        for a in range(images // CHUNK):
            part = dot(w[:, a * CHUNK : (a + 1) * CHUNK], texts_s, 0, 0)
            ip[a * 4 : a * 4 + 4] = part.astype(BF16).reshape(4, ROWS, student)

        def give_plane(d, carry):
            slot = (mine_p + d) % PLANE
            send(ip.at[slot], ri.at[d], grad_s.at[1], grad_r.at[1], me.in_plane(slot))
            return carry

        lax.fori_loop(1, PLANE, give_plane, 0)
        wait_for(tsib, grad_r.at[0])
        tc[...] = (tp[pl.ds(me.core * Z, Z)].astype(F32) + tsib[...].astype(F32)).astype(BF16)

        def give_line(d, carry):
            z = (me.z + d) % Z
            send(tc.at[z], rt.at[d], grad_s.at[2], grad_r.at[2], me.at(z=z))
            return carry

        lax.fori_loop(1, Z, give_line, 0)

        for g, (msg, kl, got, gotk, where, mine) in enumerate(groups):
            got[0] = msg[...]
            gotk[0] = kl[...]
            wait_for(gotk.at[pl.ds(1, 15)], small_r.at[1, g])
            share = jnp.exp2(got[:, 0:4, :] - lse[g][None, 0:4, :])
            kl_sum = jnp.sum(gotk[:, 0:4, :] * share, axis=0)
            loss = (kl_sum - lse[g][0:4] + lse[g][4:8]) * math.log(2.0)
            out = (row_out, col_out)[g]
            out[...] = jnp.concatenate([loss, loss], axis=0)

        ri[0] = ip[mine_p]
        rt[0] = tc[me.z]
        wait_for(ri.at[pl.ds(1, 15)], grad_r.at[1])
        image_out[...] = jnp.sum(ri[...].astype(F32), axis=0)
        wait_for(rt.at[pl.ds(1, 7)], grad_r.at[2])
        text_out[...] = jnp.sum(rt[...].astype(F32), axis=0)
        wait_for(tsib, grad_s.at[0])
        wait_for(ri.at[pl.ds(1, 15)], grad_s.at[1])
        wait_for(rt.at[pl.ds(1, 7)], grad_s.at[2])

    if stage >= 3:
        for g, (msg, kl, got, gotk, where, mine) in enumerate(groups):
            if stage == 3:
                wait_for(gotk.at[pl.ds(1, 15)], small_r.at[1, g])
            wait_for(got.at[pl.ds(1, 15)], small_s.at[0, g])
            wait_for(gotk.at[pl.ds(1, 15)], small_s.at[1, g])
    for n, (texts_buf, image_buf) in enumerate(((tt, it), (st, is_))):
        wait_for(texts_buf.at[pl.ds(0, 15)], line_s.at[n])
        wait_for(image_buf.at[pl.ds(0, 15)], plane_s.at[n])


def body(teacher_image, teacher_text, student_image, student_text, stage=4):
    teacher, student = teacher_text.shape[1], student_text.shape[1]
    texts, images = LINE * ROWS, PLANE * ROWS
    chunks = texts // CHUNK
    vmem = pltpu.VMEM
    dma = pltpu.SemaphoreType.DMA
    outs = pl.pallas_call(
        functools.partial(kernel, stage),
        out_shape=(
            jax.ShapeDtypeStruct((ROWS, student), F32),
            jax.ShapeDtypeStruct((ROWS, student), F32),
            jax.ShapeDtypeStruct((8, 128), F32),
            jax.ShapeDtypeStruct((8, 128), F32),
        ),
        in_specs=[pl.BlockSpec(memory_space=pl.ANY)] * 4,
        out_specs=(pl.BlockSpec(memory_space=pltpu.VMEM),) * 4,
        scratch_shapes=[
            vmem((LINE, ROWS, teacher), BF16),
            vmem((LINE, ROWS, student), BF16),
            vmem((PLANE,) + teacher_image.shape, BF16),
            vmem((PLANE,) + student_image.shape, BF16),
            vmem((texts, images), F32),
            vmem((texts, images), F32),
            vmem((texts, images), F32),
            vmem((texts, images), F32),
            vmem((texts, images), F32),
            vmem((texts, images), BF16),
            vmem((2, texts, 1), F32),
            vmem((2, chunks, images), F32),
            vmem((2, chunks, images), F32),
            vmem((chunks, images), F32),
            vmem((8, 128), F32),
            vmem((8, 128), F32),
            vmem((8, 128), F32),
            vmem((8, 128), F32),
            vmem((16, 8, 128), F32),
            vmem((16, 8, 128), F32),
            vmem((16, 8, 128), F32),
            vmem((16, 8, 128), F32),
            vmem((LINE, ROWS, student), BF16),
            vmem((Z, ROWS, student), BF16),
            vmem((Z, ROWS, student), BF16),
            vmem((PLANE, ROWS, student), BF16),
            vmem((Z, ROWS, student), BF16),
            vmem((PLANE, ROWS, student), BF16),
            dma((4,)),
            dma((2,)),
            dma((2, 7)),
            dma((2,)),
            dma((2,)),
            dma((4, 12)),
            dma((2, 2)),
            dma((2, 2)),
            dma((3,)),
            dma((3,)),
        ],
        compiler_params=pltpu.CompilerParams(
            collective_id=0, has_side_effects=True, vmem_limit_bytes=48 * 1024 * 1024
        ),
        name="distill",
    )(teacher_image, teacher_text, student_image, student_text)
    image_sum, text_sum, row_tile, col_tile = outs
    blk, grp = lax.axis_index("blk"), lax.axis_index("grp")
    scale = 1.0 / math.sqrt(student)
    slot_p = (blk // LINE) * 8 + grp
    slot_l = (blk % 2) * Z + (blk // 2) % Z
    row_loss = lax.dynamic_slice(row_tile.reshape(8 * 128), (slot_p * ROWS,), (ROWS,))
    column_loss = lax.dynamic_slice(col_tile.reshape(8 * 128), (slot_l * ROWS,), (ROWS,))
    return (image_sum * scale, text_sum * scale, row_loss, column_loss)


def solution(mesh):
    in_specs = (P("grp", "blk"), P(("blk", "grp"), None), P("grp", "blk"), P(("blk", "grp"), None))
    out_specs = (
        P(("blk", "grp"), None),
        P(("blk", "grp"), None),
        P(("blk", "grp")),
        P(("blk", "grp")),
    )
    return jax.shard_map(body, mesh=mesh, in_specs=in_specs, out_specs=out_specs, check_vma=False)
```

```python
import functools
import math

import jax
import jax.numpy as jnp
from jax import lax
from jax.experimental import pallas as pl
from jax.experimental.pallas import tpu as pltpu
from jax.sharding import PartitionSpec as P

MESH = pl.DeviceIdType.MESH
X, Y, Z = 4, 4, 8
PLANE, LINE = X * Y, 2 * Z
ROWS = 32
CHUNK = 128
F32 = jnp.float32
BF16 = jnp.bfloat16


class Place:
    def __init__(self):
        blk = lax.axis_index("blk")
        grp = lax.axis_index("grp")
        self.core = blk % 2
        self.z = (blk // 2) % Z
        self.y = (blk // LINE) * 2 + grp // X
        self.x = grp % X

    def at(self, x=None, y=None, z=None, core=None):
        x = self.x if x is None else x
        y = self.y if y is None else y
        z = self.z if z is None else z
        core = self.core if core is None else core
        return ((y // 2) * LINE + z * 2 + core, (y % 2) * X + x)

    def in_plane(self, slot):
        return self.at(x=slot % X, y=slot // X)

    def in_line(self, slot):
        return self.at(z=slot % Z, core=slot // Z)


def wait_for(ref, sem):
    pltpu.make_async_copy(ref, ref, sem).wait()


def send(src, dst, send_sem, recv_sem, device):
    pltpu.make_async_remote_copy(
        src_ref=src,
        dst_ref=dst,
        send_sem=send_sem,
        recv_sem=recv_sem,
        device_id=device,
        device_id_type=MESH,
    ).start()


class Gather:
    NEAR = (2, -1, 1)

    def __init__(self, me, texts, images, send_sem, line_r, plane_r, other_r):
        self.me, self.texts, self.images = me, texts, images
        self.ss, self.line_r, self.plane_r, self.other = send_sem, line_r, plane_r, other_r

    def text(self, dz):
        me = self.me
        return self.texts.at[me.core * Z + lax.rem(me.z + dz + Z, Z)]

    def image(self, dx, dy):
        me = self.me
        return self.images.at[lax.rem(me.y + dy + Y, Y) * X + lax.rem(me.x + dx + X, X)]

    def up(self, ref, sem, by):
        me = self.me
        send(ref, ref, self.ss.at[0], self.line_r.at[sem], me.at(z=lax.rem(me.z + by + Z, Z)))

    def share(self, dz):
        ref = self.text(dz)
        send(ref, ref, self.ss.at[0], self.other, self.me.at(core=1 - self.me.core))

    def over(self, ref, sem, axis, by):
        me = self.me
        if axis == 0:
            to = me.at(x=lax.rem(me.x + by + X, X))
        else:
            to = me.at(y=lax.rem(me.y + by + Y, Y))
        send(ref, ref, self.ss.at[1], self.plane_r.at[sem], to)

    def plane_begin(self):
        own = self.image(0, 0)
        for n, by in enumerate((2, 1, -1)):
            self.over(own, n, 0, by)
            self.over(own, 3 + n, 1, by)

    def line_far(self):
        own = self.text(0)
        self.up(own, 0, 2)
        self.up(own, 1, -2)

    def line_near(self):
        own = self.text(0)
        self.up(own, 2, 1)
        self.up(own, 3, -1)
        self.share(0)

    def plane_turn(self):
        rows = self.images.shape[1] // 2
        for n, by in enumerate(self.NEAR):
            for axis in range(2):
                block = self.image(by, 0) if axis == 0 else self.image(0, by)
                wait_for(block, self.plane_r.at[3 * axis + n])
                part = block.at[pl.ds(axis * rows, rows)]
                for to in (2, 1, -1):
                    self.over(part, 6, 1 - axis, to)

    def line_turn(self):
        half = ROWS // 2
        a, b = self.text(-2), self.text(2)
        wait_for(a, self.line_r.at[0])
        wait_for(b, self.line_r.at[1])
        self.up(a.at[pl.ds(0, half)], 6, 2)
        self.up(b.at[pl.ds(half, half)], 6, -2)
        self.up(a, 4, 1)
        self.up(b, 5, -1)
        self.share(-2)
        self.share(2)
        wait_for(self.text(-1), self.line_r.at[2])
        wait_for(self.text(1), self.line_r.at[3])
        self.share(-1)
        self.share(1)

    def line_finish(self):
        wait_for(self.text(-3), self.line_r.at[4])
        wait_for(self.text(3), self.line_r.at[5])
        self.share(-3)
        self.share(3)
        wait_for(self.text(4), self.line_r.at[6])
        self.share(4)

    def finish(self):
        wait_for(self.images.at[pl.ds(0, 9)], self.plane_r.at[6])
        wait_for(self.texts.at[pl.ds((1 - self.me.core) * Z, Z)], self.other)

    def end(self):
        wait_for(self.texts.at[pl.ds(0, 15)], self.ss.at[0])
        wait_for(self.images.at[pl.ds(0, 15)], self.ss.at[1])


def diagonal():
    rows = lax.broadcasted_iota(jnp.int32, (CHUNK, CHUNK), 0)
    cols = lax.broadcasted_iota(jnp.int32, (CHUNK, CHUNK), 1)
    return rows == cols


def to_lanes(column):
    return jnp.sum(jnp.where(diagonal(), column, 0.0), axis=0, keepdims=True)


def to_rows(lanes):
    return jnp.sum(jnp.where(diagonal(), lanes, 0.0), axis=1, keepdims=True)


def dot(a, b, ca, cb):
    return lax.dot_general(a, b, (((ca,), (cb,)), ((), ())), preferred_element_type=F32)


def across(parts):
    return jnp.concatenate(parts, axis=1)


def kernel(
    stage,
    ti_hbm, tt_hbm, si_hbm, st_hbm,
    image_out, text_out, row_out, col_out,
    tt, st, it, is_, s2, ert, ect, ers, ecs, w, col_max, row_max, row_sum, row_kl,
    s_line, s_plane, t_line, t_plane, gs_line, gs_plane, gt_line, gt_plane, col_lse,
    tp, tsend, tsib, tc, ip, rt, ri,
    local_sem, gather_sem, line_r, plane_r, other_r,
    small_s, small_r, sib_s, sib_r, grad_s, grad_r,
):
    me = Place()
    texts, images = LINE * ROWS, PLANE * ROWS
    teacher, student = tt.shape[2], st.shape[2]
    pairs = float(images * LINE)
    chunks = texts // CHUNK
    cut = CHUNK // ROWS
    mine_p = me.y * X + me.x
    mine_l = me.core * Z + me.z

    own = [
        pltpu.make_async_copy(tt_hbm, tt.at[mine_l], local_sem.at[0]),
        pltpu.make_async_copy(ti_hbm, it.at[mine_p], local_sem.at[1]),
        pltpu.make_async_copy(st_hbm, st.at[mine_l], local_sem.at[2]),
        pltpu.make_async_copy(si_hbm, is_.at[mine_p], local_sem.at[3]),
    ]
    for copy in own:
        copy.start()
    barrier = pltpu.get_barrier_semaphore()

    near = [me.at(core=1 - me.core)]
    near += [me.at(z=lax.rem(me.z + dz, Z)) for dz in (1, 2, Z - 2, Z - 1)]
    near += [me.at(x=lax.rem(me.x + d, X)) for d in range(1, X)]
    near += [me.at(y=lax.rem(me.y + d, Y)) for d in range(1, Y)]
    for device in near:
        pl.semaphore_signal(barrier, inc=1, device_id=device, device_id_type=MESH)
    for copy in own:
        copy.wait()
    pl.semaphore_wait(barrier, len(near))

    teacher_in = Gather(me, tt, it, gather_sem.at[0], line_r.at[0], plane_r.at[0], other_r.at[0])
    student_in = Gather(me, st, is_, gather_sem.at[1], line_r.at[1], plane_r.at[1], other_r.at[1])
    both = (student_in, teacher_in)
    for g in both:
        g.line_far()
        g.plane_begin()
    for g in both:
        g.line_near()
    for g in both:
        g.plane_turn()
        g.line_turn()

    def tiles_of(k, texts_buf, image_buf):
        width = texts_buf.shape[2]
        scale = math.log2(math.e) / math.sqrt(width)
        block = texts_buf[pl.ds(k * cut, cut)].reshape(CHUNK, width)
        return [dot(block, image_buf[pl.ds(a * 8, 8)].reshape(width, 256), 1, 0) * scale for a in range(images // 256)]

    def stats(k, which, tiles, er, ec, seen):
        rows = pl.ds(pl.multiple_of(k * CHUNK, CHUNK), CHUNK)
        top = jnp.max(functools.reduce(jnp.maximum, tiles), axis=1, keepdims=True)
        col_max[which, rows] = top
        sums = []
        for a, tile in enumerate(tiles):
            cols = pl.ds(a * 256, 256)
            e_col = jnp.exp2(tile - top)
            ec[rows, cols] = e_col
            sums.append(e_col)
            high = jnp.max(tile, axis=0, keepdims=True)
            e_row = jnp.exp2(tile - high)
            er[rows, cols] = e_row
            row_max[which, pl.ds(k, 1), cols] = high
            row_sum[which, pl.ds(k, 1), cols] = jnp.sum(e_row, axis=0, keepdims=True)
            seen(rows, cols, tile, e_row, e_col)
        total = jnp.sum(functools.reduce(jnp.add, sums), axis=1, keepdims=True)
        return top + jnp.log2(total), total

    def row_stats(which):
        high = row_max[which]
        top = jnp.max(high, axis=0, keepdims=True)
        part = jnp.exp2(high - top)
        total = jnp.sum(row_sum[which] * part, axis=0, keepdims=True)
        return top + jnp.log2(total), part, total

    def lay(ref, first, lanes):
        for a in range(4):
            ref[first + a : first + a + 1, :] = lanes[:, a * 128 : a * 128 + 128]

    groups = (me.in_plane, mine_p, (s_plane, gs_plane), (t_plane, gt_plane)), (
        me.in_line, mine_l, (s_line, gs_line), (t_line, gt_line))

    def tell(n):
        def one(d, carry):
            for g, (where, mine, *pair) in enumerate(groups):
                msg, got = pair[n]
                send(msg, got.at[d], small_s.at[n, g], small_r.at[n, g], where((mine + d) % 16))
            return carry

        lax.fori_loop(1, 16, one, 0)

    def hear(n, g):
        msg, got = groups[g][2 + n]
        got[0] = msg[...]
        wait_for(got.at[pl.ds(1, 15)], small_r.at[n, g])
        every = got[:, 0:4, :]
        top = jnp.max(every, axis=0)
        return top + jnp.log2(jnp.sum(jnp.exp2(every - top[None]), axis=0))

    student_in.line_finish()
    student_in.finish()
    if stage >= 2:

        def student_chunk(k, carry):
            tiles = tiles_of(k, st, is_)

            def seen(rows, cols, tile, e_row, e_col):
                s2[rows, cols] = tile

            lse, _ = stats(k, 1, tiles, ers, ecs, seen)
            s_line[pl.ds(k, 1), :] = to_lanes(lse)
            return carry

        lax.fori_loop(0, chunks, student_chunk, 0)
        lay(s_plane, 0, row_stats(1)[0])
    if stage >= 3:
        tell(0)
    teacher_in.line_finish()
    teacher_in.finish()
    if stage >= 2:

        def teacher_chunk(k, carry):
            tiles = tiles_of(k, tt, it)
            kls = []

            def seen(rows, cols, tile, e_row, e_col):
                gap = tile - s2[rows, cols]
                kls.append(e_col * gap)
                row_kl[pl.ds(k, 1), cols] = jnp.sum(e_row * gap, axis=0, keepdims=True)

            lse, total = stats(k, 0, tiles, ert, ect, seen)
            t_line[pl.ds(k, 1), :] = to_lanes(lse)
            kl = jnp.sum(functools.reduce(jnp.add, kls), axis=1, keepdims=True)
            t_line[pl.ds(4 + k, 1), :] = to_lanes(kl / total)
            return carry

        lax.fori_loop(0, chunks, teacher_chunk, 0)
        lse, part, total = row_stats(0)
        lay(t_plane, 0, lse)
        lay(t_plane, 4, jnp.sum(row_kl[...] * part, axis=0, keepdims=True) / total)
    if stage >= 3:
        tell(1)
        lse_s = [hear(0, 0), hear(0, 1)]
        if stage >= 4:
            image_lse = across([lse_s[0][a : a + 1, :] for a in range(4)])
            col_lse[...] = lse_s[1]

            def student_part(k, carry):
                rows = pl.ds(pl.multiple_of(k * CHUNK, CHUNK), CHUNK)
                by_row = jnp.exp2(row_max[1, pl.ds(k, 1), :] - image_lse) * pairs
                by_col = jnp.exp2(col_max[1, rows] - to_rows(col_lse[pl.ds(k, 1), :])) * pairs
                ers[rows, :] = ers[rows, :] * by_row + ecs[rows, :] * by_col
                return carry

            lax.fori_loop(0, chunks, student_part, 0)
        lse_t = [hear(1, 0), hear(1, 1)]

    if stage >= 4:
        image_lse = across([lse_t[0][a : a + 1, :] for a in range(4)])
        col_lse[...] = lse_t[1]
        other = 1 - me.core

        def weigh(k):
            rows = pl.ds(pl.multiple_of(k * CHUNK, CHUNK), CHUNK)
            by_row = jnp.exp2(row_max[0, pl.ds(k, 1), :] - image_lse) * pairs
            by_col = jnp.exp2(col_max[0, rows] - to_rows(col_lse[pl.ds(k, 1), :])) * pairs
            weights = (ers[rows, :] - ert[rows, :] * by_row - ect[rows, :] * by_col).astype(BF16)
            w[rows, :] = weights
            parts = [
                dot(weights[:, a * 256 : a * 256 + 256], is_[pl.ds(a * 8, 8)].reshape(student, 256), 1, 1)
                for a in range(images // 256)
            ]
            return functools.reduce(jnp.add, parts).reshape(cut, ROWS, student)

        half = lax.div(me.z, 4)

        def part_of(n):
            h = lax.rem(half + 1 + n, 2)
            return h, pl.ds(h * cut, cut)

        for n in range(2):
            h, part = part_of(n)
            tsend[part] = weigh(other * 2 + h).astype(BF16)
            send(tsend.at[part], tsib.at[part], sib_s.at[n], sib_r.at[n], me.at(core=other))
        for n in range(2):
            h, part = part_of(n)
            tp[part] = weigh(me.core * 2 + h)

        def give_line(n):
            h, part = part_of(n)
            wait_for(tsib.at[part], sib_r.at[n])
            tc[part] = (tp[part] + tsib[part].astype(F32)).astype(BF16)
            for i in range(n, 4):
                z = h * 4 + lax.rem(me.z + i, 4)
                d = lax.rem(z - me.z + Z, Z)
                send(tc.at[z], rt.at[d], grad_s.at[1], grad_r.at[1], me.at(z=z))

        def give_plane(dy):
            y = lax.rem(me.y + dy, Y)
            block = w[:, pl.ds(pl.multiple_of(y * CHUNK, CHUNK), CHUNK)]
            part = dot(block, st[...].reshape(texts, student), 0, 0)
            ip[pl.ds(y * X, X)] = part.astype(BF16).reshape(X, ROWS, student)
            for dx in (2, 1, 3, 0):
                if dx or dy:
                    slot = y * X + lax.rem(me.x + dx, X)
                    send(ip.at[slot], ri.at[dy * X + dx], grad_s.at[0], grad_r.at[0], me.in_plane(slot))

        give_plane(2)
        give_line(0)
        give_plane(1)
        give_line(1)
        give_plane(3)
        give_plane(0)

        for g, (where, mine, _, (msg, got)) in enumerate(groups):
            share = jnp.exp2(got[:, 0:4, :] - lse_t[g][None])
            loss = jnp.sum(got[:, 4:8, :] * share, axis=0) - lse_t[g] + lse_s[g]
            picked = lax.broadcasted_iota(jnp.int32, loss.shape, 0) == lax.div(mine, 4)
            row = jnp.sum(jnp.where(picked, loss, 0.0), axis=0, keepdims=True)
            turned = pltpu.roll(jnp.broadcast_to(row, (8, 128)), lax.rem(128 - lax.rem(mine, 4) * ROWS, 128), 1)
            (row_out, col_out)[g][...] = turned

        ri[0] = ip[mine_p]
        rt[0] = tc[me.z]
        wait_for(ri.at[pl.ds(1, PLANE - 1)], grad_r.at[0])
        image_out[...] = jnp.sum(ri[...].astype(F32), axis=0)
        wait_for(rt.at[pl.ds(1, Z - 1)], grad_r.at[1])
        text_out[...] = jnp.sum(rt[...].astype(F32), axis=0)
        for n in range(2):
            wait_for(tsib.at[pl.ds(0, cut)], sib_s.at[n])
        wait_for(ri.at[pl.ds(1, PLANE - 1)], grad_s.at[0])
        wait_for(rt.at[pl.ds(1, Z - 1)], grad_s.at[1])

    if stage >= 3:
        for g, (where, mine, *pair) in enumerate(groups):
            for n in range(2):
                wait_for(pair[n][1].at[pl.ds(1, 15)], small_s.at[n, g])
    student_in.end()
    teacher_in.end()


def body(teacher_image, teacher_text, student_image, student_text, stage=4):
    teacher, student = teacher_text.shape[1], student_text.shape[1]
    texts, images = LINE * ROWS, PLANE * ROWS
    chunks = texts // CHUNK
    vmem = pltpu.VMEM
    dma = pltpu.SemaphoreType.DMA
    tile = vmem((texts, images), F32)
    grads = vmem((Z, ROWS, student), BF16)
    args = (teacher_image, teacher_text, student_image, student_text)
    image_sum, text_sum, row, col = pl.pallas_call(
        functools.partial(kernel, stage),
        out_shape=(
            jax.ShapeDtypeStruct((ROWS, student), F32),
            jax.ShapeDtypeStruct((ROWS, student), F32),
            jax.ShapeDtypeStruct((8, 128), F32),
            jax.ShapeDtypeStruct((8, 128), F32),
        ),
        in_specs=[pl.BlockSpec(memory_space=pltpu.HBM)] * 4,
        out_specs=(pl.BlockSpec(memory_space=pltpu.VMEM),) * 4,
        scratch_shapes=[
            vmem((LINE, ROWS, teacher), BF16),
            vmem((LINE, ROWS, student), BF16),
            vmem((PLANE,) + teacher_image.shape, BF16),
            vmem((PLANE,) + student_image.shape, BF16),
            tile,
            tile,
            tile,
            tile,
            tile,
            vmem((texts, images), BF16),
            vmem((2, texts, 1), F32),
            vmem((2, chunks, images), F32),
            vmem((2, chunks, images), F32),
            vmem((chunks, images), F32),
            vmem((4, 128), F32),
            vmem((4, 128), F32),
            vmem((8, 128), F32),
            vmem((8, 128), F32),
            vmem((16, 4, 128), F32),
            vmem((16, 4, 128), F32),
            vmem((16, 8, 128), F32),
            vmem((16, 8, 128), F32),
            vmem((4, 128), F32),
            vmem((Z, ROWS, student), F32),
            grads,
            grads,
            grads,
            vmem((PLANE, ROWS, student), BF16),
            grads,
            vmem((PLANE, ROWS, student), BF16),
            dma((4,)),
            dma((2, 2)),
            dma((2, 7)),
            dma((2, 7)),
            dma((2,)),
            dma((2, 2)),
            dma((2, 2)),
            dma((2,)),
            dma((2,)),
            dma((2,)),
            dma((2,)),
        ],
        compiler_params=pltpu.CompilerParams(
            collective_id=0, has_side_effects=True, vmem_limit_bytes=40 * 1024 * 1024
        ),
        name="distill",
    )(*[pltpu.with_memory_space_constraint(a, pltpu.HBM) for a in args])
    scale = 1.0 / math.sqrt(student)
    log2 = math.log(2.0)
    return (image_sum * scale, text_sum * scale, row[0, :ROWS] * log2, col[0, :ROWS] * log2)


def solution(mesh):
    in_specs = (P("grp", "blk"), P(("blk", "grp"), None), P("grp", "blk"), P(("blk", "grp"), None))
    out_specs = (
        P(("blk", "grp"), None),
        P(("blk", "grp"), None),
        P(("blk", "grp")),
        P(("blk", "grp")),
    )
    return jax.shard_map(body, mesh=mesh, in_specs=in_specs, out_specs=out_specs, check_vma=False)
```

```python
import functools
import math

import jax
import jax.numpy as jnp
from jax import lax
from jax.experimental import pallas as pl
from jax.experimental.pallas import tpu as pltpu
from jax.sharding import PartitionSpec as P

MESH = pl.DeviceIdType.MESH
X, Y, Z = 4, 4, 8
PLANE, LINE = X * Y, 2 * Z
ROWS = 32
CHUNK = 128
F32 = jnp.float32
BF16 = jnp.bfloat16


class Place:
    def __init__(self):
        blk = lax.axis_index("blk")
        grp = lax.axis_index("grp")
        self.core = blk % 2
        self.z = (blk // 2) % Z
        self.y = (blk // LINE) * 2 + grp // X
        self.x = grp % X

    def at(self, x=None, y=None, z=None, core=None):
        x = self.x if x is None else x
        y = self.y if y is None else y
        z = self.z if z is None else z
        core = self.core if core is None else core
        return ((y // 2) * LINE + z * 2 + core, (y % 2) * X + x)

    def in_plane(self, slot):
        return self.at(x=slot % X, y=slot // X)

    def in_line(self, slot):
        return self.at(z=slot % Z, core=slot // Z)


def far(by, size):
    return min(by, size - by)


def wait_for(ref, sem):
    pltpu.make_async_copy(ref, ref, sem).wait()


def send(src, dst, send_sem, recv_sem, device):
    pltpu.make_async_remote_copy(
        src_ref=src,
        dst_ref=dst,
        send_sem=send_sem,
        recv_sem=recv_sem,
        device_id=device,
        device_id_type=MESH,
    ).start()


class Gather:
    NEAR = (2, -1, 1)

    def __init__(self, me, own_texts, own_images, texts, images, send_sem, line_r, plane_r, other_r):
        self.me, self.texts, self.images = me, texts, images
        self.own_texts, self.own_images = own_texts, own_images
        self.ss, self.line_r, self.plane_r, self.other = send_sem, line_r, plane_r, other_r

    def text(self, dz):
        me = self.me
        return self.texts.at[me.core * Z + lax.rem(me.z + dz + Z, Z)]

    def image(self, dx, dy):
        me = self.me
        return self.images.at[lax.rem(me.y + dy + Y, Y) * X + lax.rem(me.x + dx + X, X)]

    def up(self, ref, sem, by, src=None):
        me = self.me
        send(ref if src is None else src, ref, self.ss.at[0], self.line_r.at[sem], me.at(z=lax.rem(me.z + by + Z, Z)))

    def share(self, dz, src=None):
        ref = self.text(dz)
        send(ref if src is None else src, ref, self.ss.at[0], self.other, self.me.at(core=1 - self.me.core))

    def over(self, ref, sem, axis, by, src=None):
        me = self.me
        if axis == 0:
            to = me.at(x=lax.rem(me.x + by + X, X))
        else:
            to = me.at(y=lax.rem(me.y + by + Y, Y))
        send(ref if src is None else src, ref, self.ss.at[1], self.plane_r.at[sem], to)

    def part(self, block, axis):
        rows = self.images.shape[1] // 2
        return block.at[pl.ds(axis * rows, rows)]

    def plane_begin(self):
        own = self.image(0, 0)
        for n, by in enumerate((2, 1, -1)):
            for axis in range(2):
                self.over(self.part(own, axis), 3 * axis + n, axis, by, self.part(self.own_images, axis))

    def plane_rest(self):
        own = self.image(0, 0)
        for by in (2, 1, -1):
            for axis in range(2):
                self.over(self.part(own, 1 - axis), 6, axis, by, self.part(self.own_images, 1 - axis))

    def line_far(self):
        own = self.text(0)
        self.up(own, 0, 2, self.own_texts)
        self.up(own, 1, -2, self.own_texts)

    def line_near(self):
        own = self.text(0)
        self.up(own, 2, 1, self.own_texts)
        self.up(own, 3, -1, self.own_texts)
        self.share(0, self.own_texts)

    def plane_turn(self):
        for n, by in enumerate(self.NEAR):
            for axis in range(2):
                part = self.part(self.image(by, 0) if axis == 0 else self.image(0, by), axis)
                wait_for(part, self.plane_r.at[3 * axis + n])
                for to in (2, 1, -1):
                    self.over(part, 6, 1 - axis, to)

    def line_turn(self):
        half = ROWS // 2
        a, b = self.text(-2), self.text(2)
        wait_for(a, self.line_r.at[0])
        wait_for(b, self.line_r.at[1])
        self.up(a.at[pl.ds(0, half)], 6, 2)
        self.up(b.at[pl.ds(half, half)], 6, -2)
        self.up(a, 4, 1)
        self.up(b, 5, -1)
        self.share(-2)
        self.share(2)

    def line_share(self):
        wait_for(self.text(-1), self.line_r.at[2])
        wait_for(self.text(1), self.line_r.at[3])
        self.share(-1)
        self.share(1)

    def line_finish(self):
        wait_for(self.text(-3), self.line_r.at[4])
        wait_for(self.text(3), self.line_r.at[5])
        self.share(-3)
        self.share(3)
        wait_for(self.text(4), self.line_r.at[6])
        self.share(4)

    def plane_finish(self):
        wait_for(self.images.at[pl.ds(0, 12)], self.plane_r.at[6])

    def other_finish(self):
        wait_for(self.texts.at[pl.ds((1 - self.me.core) * Z, Z)], self.other)

    def end(self):
        wait_for(self.texts.at[pl.ds(0, 15)], self.ss.at[0])
        wait_for(self.images.at[pl.ds(0, 15)], self.ss.at[1])


def diagonal():
    rows = lax.broadcasted_iota(jnp.int32, (CHUNK, CHUNK), 0)
    cols = lax.broadcasted_iota(jnp.int32, (CHUNK, CHUNK), 1)
    return rows == cols


def to_lanes(column):
    return jnp.sum(jnp.where(diagonal(), column, 0.0), axis=0, keepdims=True)


def to_rows(lanes):
    return jnp.sum(jnp.where(diagonal(), lanes, 0.0), axis=1, keepdims=True)


def dot(a, b, ca, cb):
    return lax.dot_general(a, b, (((ca,), (cb,)), ((), ())), preferred_element_type=F32)


def across(parts):
    return jnp.concatenate(parts, axis=1)


def kernel(
    stage,
    ti_hbm, tt_hbm, si_hbm, st_hbm,
    image_out, text_out, row_out, col_out,
    tt, st, it, is_, s2, t2, ert, ect, ers, ecs, w, col_max, col_sum, row_max, row_sum,
    s_line, s_plane, t_line, t_plane, k_line, k_plane,
    gs_line, gs_plane, gt_line, gt_plane, gk_line, gk_plane, col_lse,
    tp, tsend, tsib, tc, ip, ip0, rt, ri,
    local_sem, gather_sem, line_r, plane_r, other_r,
    small_s, small_r, sib_s, sib_r, grad_s, grad_r,
):
    me = Place()
    texts, images = LINE * ROWS, PLANE * ROWS
    teacher, student = tt.shape[2], st.shape[2]
    pairs = float(images * LINE)
    chunks = texts // CHUNK
    cut = CHUNK // ROWS
    mine_p = me.y * X + me.x
    mine_l = me.core * Z + me.z

    own = [
        pltpu.make_async_copy(tt_hbm, tt.at[mine_l], local_sem.at[0]),
        pltpu.make_async_copy(ti_hbm, it.at[mine_p], local_sem.at[1]),
        pltpu.make_async_copy(st_hbm, st.at[mine_l], local_sem.at[2]),
        pltpu.make_async_copy(si_hbm, is_.at[mine_p], local_sem.at[3]),
    ]
    barrier = pltpu.get_barrier_semaphore()

    near = [me.at(core=1 - me.core)]
    near += [me.at(z=lax.rem(me.z + dz, Z)) for dz in (1, 2, Z - 2, Z - 1)]
    near += [me.at(x=lax.rem(me.x + d, X)) for d in range(1, X)]
    near += [me.at(y=lax.rem(me.y + d, Y)) for d in range(1, Y)]
    for device in near:
        pl.semaphore_signal(barrier, inc=1, device_id=device, device_id_type=MESH)
    for copy in own:
        copy.start()
    pl.semaphore_wait(barrier, len(near))

    teacher_in = Gather(me, tt_hbm, ti_hbm, tt, it, gather_sem.at[0], line_r.at[0], plane_r.at[0], other_r.at[0])
    student_in = Gather(me, st_hbm, si_hbm, st, is_, gather_sem.at[1], line_r.at[1], plane_r.at[1], other_r.at[1])
    both = (student_in, teacher_in)
    for g in both:
        g.line_far()
        g.plane_begin()
    for g in both:
        g.plane_rest()
        g.line_near()
    for g in both:
        g.plane_turn()
        g.line_turn()
    for g in both:
        g.line_share()
    for copy in own:
        copy.wait()

    def tiles_of(k, texts_buf, image_buf):
        width = texts_buf.shape[2]
        scale = math.log2(math.e) / math.sqrt(width)
        block = texts_buf[pl.ds(k * cut, cut)].reshape(CHUNK, width)
        return [dot(block, image_buf[pl.ds(a * 8, 8)].reshape(width, 256), 1, 0) * scale for a in range(images // 256)]

    def stats(k, which, tiles, er, ec, seen):
        rows = pl.ds(pl.multiple_of(k * CHUNK, CHUNK), CHUNK)
        top = jnp.max(functools.reduce(jnp.maximum, tiles), axis=1, keepdims=True)
        col_max[which, rows] = top
        sums = []
        for a, tile in enumerate(tiles):
            cols = pl.ds(a * 256, 256)
            e_col = jnp.exp2(tile - top)
            ec[rows, cols] = e_col
            sums.append(e_col)
            high = jnp.max(tile, axis=0, keepdims=True)
            e_row = jnp.exp2(tile - high)
            er[rows, cols] = e_row
            row_max[which, pl.ds(k, 1), cols] = high
            row_sum[which, pl.ds(k, 1), cols] = jnp.sum(e_row, axis=0, keepdims=True)
            seen(rows, cols, tile, e_row, e_col)
        total = jnp.sum(functools.reduce(jnp.add, sums), axis=1, keepdims=True)
        return top + jnp.log2(total), total

    def row_stats(which):
        high = row_max[which]
        top = jnp.max(high, axis=0, keepdims=True)
        part = jnp.exp2(high - top)
        total = jnp.sum(row_sum[which] * part, axis=0, keepdims=True)
        return top + jnp.log2(total), part, total

    def lay(ref, first, lanes):
        for a in range(4):
            ref[first + a : first + a + 1, :] = lanes[:, a * 128 : a * 128 + 128]

    planes = sorted(((dx, dy) for dx in range(X) for dy in range(Y) if dx or dy), key=lambda o: -far(o[0], X) - far(o[1], Y))
    lines = sorted(((dz, dc) for dz in range(Z) for dc in range(2) if dz or dc), key=lambda o: -far(o[0], Z))
    groups = ((s_plane, gs_plane), (t_plane, gt_plane), (k_plane, gk_plane)), (
        (s_line, gs_line), (t_line, gt_line), (k_line, gk_line))

    def tell(n):
        for (dx, dy), (dz, dc) in zip(planes, lines):
            msg, got = groups[0][n]
            to = me.at(x=lax.rem(me.x + dx, X), y=lax.rem(me.y + dy, Y))
            send(msg, got.at[dy * X + dx], small_s.at[n, 0], small_r.at[n, 0], to)
            msg, got = groups[1][n]
            to = me.at(z=lax.rem(me.z + dz, Z), core=lax.rem(me.core + dc, 2))
            send(msg, got.at[dc * Z + dz], small_s.at[n, 1], small_r.at[n, 1], to)

    def hear(n, g):
        msg, got = groups[g][n]
        got[0] = msg[...]
        wait_for(got.at[pl.ds(1, 15)], small_r.at[n, g])
        every = got[...]
        top = jnp.max(every, axis=0)
        return top + jnp.log2(jnp.sum(jnp.exp2(every - top[None]), axis=0))

    def by_core(source, step):
        per_core = chunks // 2
        for core in (me.core, 1 - me.core):
            for k in range(per_core):
                step(core * per_core + k)
            if core is me.core:
                source.other_finish()

    student_in.line_finish()
    student_in.plane_finish()
    if stage >= 2:

        def student_chunk(k):
            tiles = tiles_of(k, st, is_)

            def seen(rows, cols, tile, e_row, e_col):
                s2[rows, cols] = tile

            lse, _ = stats(k, 1, tiles, ers, ecs, seen)
            s_line[pl.ds(k, 1), :] = to_lanes(lse)

        by_core(student_in, student_chunk)
        lay(s_plane, 0, row_stats(1)[0])
    if stage >= 3:
        tell(0)
    teacher_in.line_finish()
    teacher_in.plane_finish()
    if stage >= 2:

        def teacher_chunk(k):
            tiles = tiles_of(k, tt, it)

            def seen(rows, cols, tile, e_row, e_col):
                t2[rows, cols] = tile

            lse, total = stats(k, 0, tiles, ert, ect, seen)
            col_sum[pl.ds(pl.multiple_of(k * CHUNK, CHUNK), CHUNK)] = total
            t_line[pl.ds(k, 1), :] = to_lanes(lse)

        by_core(teacher_in, teacher_chunk)
        lse, part, total = row_stats(0)
        lay(t_plane, 0, lse)
    if stage >= 3:
        tell(1)
        row_kl = jnp.zeros((1, images), F32)
        for k in range(chunks):
            rows = pl.ds(k * CHUNK, CHUNK)
            gap = t2[rows, :] - s2[rows, :]
            row_kl += jnp.sum(ert[rows, :] * gap, axis=0, keepdims=True) * part[k : k + 1, :]
            kl = jnp.sum(ect[rows, :] * gap, axis=1, keepdims=True) / col_sum[rows]
            k_line[pl.ds(k, 1), :] = to_lanes(kl)
        lay(k_plane, 0, row_kl / total)
        tell(2)
        lse_s = [hear(0, 0), hear(0, 1)]
        if stage >= 4:
            image_lse = across([lse_s[0][a : a + 1, :] for a in range(4)])
            col_lse[...] = lse_s[1]

            def student_part(k, carry):
                rows = pl.ds(pl.multiple_of(k * CHUNK, CHUNK), CHUNK)
                by_row = jnp.exp2(row_max[1, pl.ds(k, 1), :] - image_lse) * pairs
                by_col = jnp.exp2(col_max[1, rows] - to_rows(col_lse[pl.ds(k, 1), :])) * pairs
                ers[rows, :] = ers[rows, :] * by_row + ecs[rows, :] * by_col
                return carry

            lax.fori_loop(0, chunks, student_part, 0)
        lse_t = [hear(1, 0), hear(1, 1)]

    if stage >= 4:
        image_lse = across([lse_t[0][a : a + 1, :] for a in range(4)])
        col_lse[...] = lse_t[1]
        other = 1 - me.core

        def weigh(k):
            rows = pl.ds(pl.multiple_of(k * CHUNK, CHUNK), CHUNK)
            by_row = jnp.exp2(row_max[0, pl.ds(k, 1), :] - image_lse) * pairs
            by_col = jnp.exp2(col_max[0, rows] - to_rows(col_lse[pl.ds(k, 1), :])) * pairs
            w[rows, :] = (ers[rows, :] - ert[rows, :] * by_row - ect[rows, :] * by_col).astype(BF16)

        def text_part(k):
            rows = pl.ds(pl.multiple_of(k * CHUNK, CHUNK), CHUNK)
            parts = [
                dot(w[rows, pl.ds(a * 256, 256)], is_[pl.ds(a * 8, 8)].reshape(student, 256), 1, 1)
                for a in range(images // 256)
            ]
            return functools.reduce(jnp.add, parts).reshape(cut, ROWS, student)

        per_core = chunks // 2

        def give_line(n):
            part = pl.ds(n * cut, cut)
            wait_for(tsib.at[part], sib_r.at[n])
            tc[part] = (tp[part] + tsib[part].astype(F32)).astype(BF16)
            for z in range(n * cut, (n + 1) * cut):

                @pl.when(me.z != z)
                def _():
                    to = rt.at[lax.rem(z - me.z + Z, Z)]
                    send(tc.at[z], to, grad_s.at[1], grad_r.at[1], me.at(z=z))

        def give_plane(dy):
            y = lax.rem(me.y + dy, Y)
            block = w[:, pl.ds(pl.multiple_of(y * CHUNK, CHUNK), CHUNK)]
            part = dot(block, st[...].reshape(texts, student), 0, 0)
            ip[pl.ds(y * X, X)] = part.astype(BF16).reshape(X, ROWS, student)
            for dx in (2, 1, 3, 0):
                if dx or dy:
                    slot = y * X + lax.rem(me.x + dx, X)

                    @pl.when(jnp.logical_or(slot != 0, me.z != 0))
                    def _():
                        send(ip.at[slot], ri.at[dy * X + dx], grad_s.at[0], grad_r.at[0], me.in_plane(slot))

        def swap(n):
            part = pl.ds(n * cut, cut)
            tsend[part] = text_part(other * per_core + n).astype(BF16)
            send(tsend.at[part], tsib.at[part], sib_s.at[n], sib_r.at[n], me.at(core=other))

        def keep(n):
            tp[pl.ds(n * cut, cut)] = text_part(me.core * per_core + n)

        weigh(other * per_core)
        swap(0)
        weigh(me.core * per_core)
        weigh(other * per_core + 1)
        weigh(me.core * per_core + 1)
        @pl.when(jnp.logical_and(me.z == 0, mine_p != 0))
        def _():
            part = dot(w[:, :CHUNK], st[...].reshape(texts, student), 0, 0)
            ip0[...] = part[:ROWS].astype(BF16)
            to = ri.at[lax.rem(Y - me.y, Y) * X + lax.rem(X - me.x, X)]
            send(ip0, to, grad_s.at[0], grad_r.at[0], me.in_plane(0))

        give_plane(2)
        swap(1)
        keep(0)
        give_plane(1)
        give_line(0)
        give_plane(3)
        keep(1)
        give_plane(0)
        give_line(1)

        for g, (_, (_, got_t), (msg, got)) in enumerate(groups):
            mine = (mine_p, mine_l)[g]
            got[0] = msg[...]
            wait_for(got.at[pl.ds(1, 15)], small_r.at[2, g])
            share = jnp.exp2(got_t[...] - lse_t[g][None])
            loss = jnp.sum(got[...] * share, axis=0) - lse_t[g] + lse_s[g]
            picked = lax.broadcasted_iota(jnp.int32, loss.shape, 0) == lax.div(mine, 4)
            row = jnp.sum(jnp.where(picked, loss, 0.0), axis=0, keepdims=True)
            turned = pltpu.roll(jnp.broadcast_to(row, (8, 128)), lax.rem(128 - lax.rem(mine, 4) * ROWS, 128), 1)
            (row_out, col_out)[g][...] = turned

        ri[0] = ip[mine_p]
        rt[0] = tc[me.z]
        wait_for(ri.at[pl.ds(1, PLANE - 1)], grad_r.at[0])
        image_out[...] = jnp.sum(ri[...].astype(F32), axis=0)
        wait_for(rt.at[pl.ds(1, Z - 1)], grad_r.at[1])
        text_out[...] = jnp.sum(rt[...].astype(F32), axis=0)
        for n in range(2):
            wait_for(tsib.at[pl.ds(0, cut)], sib_s.at[n])
        wait_for(ri.at[pl.ds(1, PLANE - 1)], grad_s.at[0])
        wait_for(rt.at[pl.ds(1, Z - 1)], grad_s.at[1])

    if stage == 1:
        student_in.other_finish()
        teacher_in.other_finish()
    if stage >= 3:
        for g in range(2):
            for n in range(3):
                wait_for(groups[g][n][1].at[pl.ds(1, 15)], small_s.at[n, g])
            if stage == 3:
                wait_for(groups[g][2][1].at[pl.ds(1, 15)], small_r.at[2, g])
    student_in.end()
    teacher_in.end()


def body(teacher_image, teacher_text, student_image, student_text, stage=4):
    teacher, student = teacher_text.shape[1], student_text.shape[1]
    texts, images = LINE * ROWS, PLANE * ROWS
    chunks = texts // CHUNK
    vmem = pltpu.VMEM
    dma = pltpu.SemaphoreType.DMA
    tile = vmem((texts, images), F32)
    grads = vmem((Z, ROWS, student), BF16)
    args = (teacher_image, teacher_text, student_image, student_text)
    image_sum, text_sum, row, col = pl.pallas_call(
        functools.partial(kernel, stage),
        out_shape=(
            jax.ShapeDtypeStruct((ROWS, student), F32),
            jax.ShapeDtypeStruct((ROWS, student), F32),
            jax.ShapeDtypeStruct((8, 128), F32),
            jax.ShapeDtypeStruct((8, 128), F32),
        ),
        in_specs=[pl.BlockSpec(memory_space=pltpu.HBM)] * 4,
        out_specs=(pl.BlockSpec(memory_space=pltpu.VMEM),) * 4,
        scratch_shapes=[
            vmem((LINE, ROWS, teacher), BF16),
            vmem((LINE, ROWS, student), BF16),
            vmem((PLANE,) + teacher_image.shape, BF16),
            vmem((PLANE,) + student_image.shape, BF16),
            tile,
            tile,
            tile,
            tile,
            tile,
            tile,
            vmem((texts, images), BF16),
            vmem((2, texts, 1), F32),
            vmem((texts, 1), F32),
            vmem((2, chunks, images), F32),
            vmem((2, chunks, images), F32),
            *[vmem((4, 128), F32)] * 6,
            *[vmem((16, 4, 128), F32)] * 6,
            vmem((4, 128), F32),
            vmem((Z, ROWS, student), F32),
            grads,
            grads,
            grads,
            vmem((PLANE, ROWS, student), BF16),
            vmem((ROWS, student), BF16),
            grads,
            vmem((PLANE, ROWS, student), BF16),
            dma((4,)),
            dma((2, 2)),
            dma((2, 7)),
            dma((2, 7)),
            dma((2,)),
            dma((3, 2)),
            dma((3, 2)),
            dma((2,)),
            dma((2,)),
            dma((2,)),
            dma((2,)),
        ],
        compiler_params=pltpu.CompilerParams(
            collective_id=0, has_side_effects=True, vmem_limit_bytes=40 * 1024 * 1024
        ),
        name="distill",
    )(*[pltpu.with_memory_space_constraint(a, pltpu.HBM) for a in args])
    scale = 1.0 / math.sqrt(student)
    log2 = math.log(2.0)
    return (image_sum * scale, text_sum * scale, row[0, :ROWS] * log2, col[0, :ROWS] * log2)


def solution(mesh):
    in_specs = (P("grp", "blk"), P(("blk", "grp"), None), P("grp", "blk"), P(("blk", "grp"), None))
    out_specs = (
        P(("blk", "grp"), None),
        P(("blk", "grp"), None),
        P(("blk", "grp")),
        P(("blk", "grp")),
    )
    return jax.shard_map(body, mesh=mesh, in_specs=in_specs, out_specs=out_specs, check_vma=False)
```

```python
import functools
import math

import jax
import jax.numpy as jnp
from jax import lax
from jax.experimental import pallas as pl
from jax.experimental.pallas import tpu as pltpu
from jax.sharding import PartitionSpec as P

MESH = pl.DeviceIdType.MESH
X, Y, Z = 4, 4, 8
PLANE, LINE = X * Y, 2 * Z
ROWS = 32
CHUNK = 128
F32 = jnp.float32
BF16 = jnp.bfloat16


class Place:
    def __init__(self):
        blk = lax.axis_index("blk")
        grp = lax.axis_index("grp")
        self.core = blk % 2
        self.z = (blk // 2) % Z
        self.y = (blk // LINE) * 2 + grp // X
        self.x = grp % X

    def at(self, x=None, y=None, z=None, core=None):
        x = self.x if x is None else x
        y = self.y if y is None else y
        z = self.z if z is None else z
        core = self.core if core is None else core
        return ((y // 2) * LINE + z * 2 + core, (y % 2) * X + x)

    def in_plane(self, slot):
        return self.at(x=slot % X, y=slot // X)

    def in_line(self, slot):
        return self.at(z=slot % Z, core=slot // Z)


def far(by, size):
    return min(by, size - by)


def wait_for(ref, sem):
    pltpu.make_async_copy(ref, ref, sem).wait()


def send(src, dst, send_sem, recv_sem, device):
    pltpu.make_async_remote_copy(
        src_ref=src,
        dst_ref=dst,
        send_sem=send_sem,
        recv_sem=recv_sem,
        device_id=device,
        device_id_type=MESH,
    ).start()


class Gather:
    NEAR = (2, -1, 1)

    def __init__(self, me, own_texts, own_images, texts, images, send_sem, line_r, plane_r, other_r):
        self.me, self.texts, self.images = me, texts, images
        self.own_texts, self.own_images = own_texts, own_images
        self.ss, self.line_r, self.plane_r, self.other = send_sem, line_r, plane_r, other_r

    def text(self, dz):
        me = self.me
        return self.texts.at[me.core * Z + lax.rem(me.z + dz + Z, Z)]

    def image(self, dx, dy):
        me = self.me
        return self.images.at[lax.rem(me.y + dy + Y, Y) * X + lax.rem(me.x + dx + X, X)]

    def up(self, ref, sem, by, src=None):
        me = self.me
        send(ref if src is None else src, ref, self.ss.at[0], self.line_r.at[sem], me.at(z=lax.rem(me.z + by + Z, Z)))

    def share(self, dz, src=None):
        ref = self.text(dz)
        send(ref if src is None else src, ref, self.ss.at[0], self.other, self.me.at(core=1 - self.me.core))

    def over(self, ref, sem, axis, by, src=None):
        me = self.me
        if axis == 0:
            to = me.at(x=lax.rem(me.x + by + X, X))
        else:
            to = me.at(y=lax.rem(me.y + by + Y, Y))
        send(ref if src is None else src, ref, self.ss.at[1], self.plane_r.at[sem], to)

    def part(self, block, axis):
        rows = self.images.shape[1] // 2
        return block.at[pl.ds(axis * rows, rows)]

    def plane_begin(self):
        own = self.image(0, 0)
        for n, by in enumerate((2, 1, -1)):
            for axis in range(2):
                self.over(self.part(own, axis), 3 * axis + n, axis, by, self.part(self.own_images, axis))

    def plane_rest(self):
        own = self.image(0, 0)
        for by in (2, 1, -1):
            for axis in range(2):
                self.over(self.part(own, 1 - axis), 6, axis, by, self.part(self.own_images, 1 - axis))

    def halves(self, block):
        half = ROWS // 2
        return block.at[pl.ds(0, half)], block.at[pl.ds(half, half)]

    def line_far(self):
        first, second = self.halves(self.text(0))
        own_first, own_second = self.halves(self.own_texts)
        self.up(first, 0, 2, own_first)
        self.up(second, 1, -2, own_second)
        self.up(second, 7, 2, own_second)
        self.up(first, 8, -2, own_first)

    def line_near(self):
        own = self.text(0)
        self.up(own, 2, 1, self.own_texts)
        self.up(own, 3, -1, self.own_texts)
        self.share(0, self.own_texts)

    def plane_turn(self):
        for n, by in enumerate(self.NEAR):
            for axis in range(2):
                part = self.part(self.image(by, 0) if axis == 0 else self.image(0, by), axis)
                wait_for(part, self.plane_r.at[3 * axis + n])
                for to in (2, 1, -1):
                    self.over(part, 6, 1 - axis, to)

    def line_next(self):
        a, b = self.text(-1), self.text(1)
        wait_for(a, self.line_r.at[2])
        wait_for(b, self.line_r.at[3])
        self.up(a, 0, 1)
        self.up(b, 1, -1)
        self.share(-1)
        self.share(1)

    def line_turn(self, halves):
        a, b = self.text(-2), self.text(2)
        first, second = self.halves(a)[0], self.halves(b)[1]
        wait_for(first if halves else a, self.line_r.at[0])
        self.up(first, 6, 2)
        wait_for(second if halves else b, self.line_r.at[1])
        self.up(second, 6, -2)

    def line_last(self, halves):
        a, b = self.text(-2), self.text(2)
        if halves:
            wait_for(self.halves(a)[1], self.line_r.at[7])
            wait_for(self.halves(b)[0], self.line_r.at[8])
        self.up(a, 4, 1)
        self.up(b, 5, -1)
        self.share(-2)
        self.share(2)

    def line_share(self):
        wait_for(self.text(-1), self.line_r.at[2])
        wait_for(self.text(1), self.line_r.at[3])
        self.share(-1)
        self.share(1)

    def line_finish(self):
        wait_for(self.text(-3), self.line_r.at[4])
        wait_for(self.text(3), self.line_r.at[5])
        self.share(-3)
        self.share(3)
        wait_for(self.text(4), self.line_r.at[6])
        self.share(4)

    def plane_finish(self):
        wait_for(self.images.at[pl.ds(0, 12)], self.plane_r.at[6])

    def other_finish(self):
        wait_for(self.texts.at[pl.ds((1 - self.me.core) * Z, Z)], self.other)

    def end(self):
        wait_for(self.texts.at[pl.ds(0, 15)], self.ss.at[0])
        wait_for(self.images.at[pl.ds(0, 15)], self.ss.at[1])


def diagonal():
    rows = lax.broadcasted_iota(jnp.int32, (CHUNK, CHUNK), 0)
    cols = lax.broadcasted_iota(jnp.int32, (CHUNK, CHUNK), 1)
    return rows == cols


def to_lanes(column):
    return jnp.sum(jnp.where(diagonal(), column, 0.0), axis=0, keepdims=True)


def to_rows(lanes):
    return jnp.sum(jnp.where(diagonal(), lanes, 0.0), axis=1, keepdims=True)


def dot(a, b, ca, cb):
    return lax.dot_general(a, b, (((ca,), (cb,)), ((), ())), preferred_element_type=F32)


def across(parts):
    return jnp.concatenate(parts, axis=1)


def kernel(
    stage,
    ti_hbm, tt_hbm, si_hbm, st_hbm,
    image_out, text_out, row_out, col_out,
    tt, st, it, is_, s2, t2, ert, ect, ers, ecs, w, col_max, col_sum, row_max, row_sum,
    s_line, s_plane, t_line, t_plane, k_line, k_plane,
    gs_line, gs_plane, gt_line, gt_plane, gk_line, gk_plane, col_lse,
    tp, tsend, tsib, tc, ip, ip0, rt, ri,
    local_sem, gather_sem, line_r, plane_r, other_r,
    small_s, small_r, sib_s, sib_r, grad_s, grad_r,
):
    me = Place()
    texts, images = LINE * ROWS, PLANE * ROWS
    teacher, student = tt.shape[2], st.shape[2]
    pairs = float(images * LINE)
    chunks = texts // CHUNK
    cut = CHUNK // ROWS
    mine_p = me.y * X + me.x
    mine_l = me.core * Z + me.z

    own = [
        pltpu.make_async_copy(tt_hbm, tt.at[mine_l], local_sem.at[0]),
        pltpu.make_async_copy(ti_hbm, it.at[mine_p], local_sem.at[1]),
        pltpu.make_async_copy(st_hbm, st.at[mine_l], local_sem.at[2]),
        pltpu.make_async_copy(si_hbm, is_.at[mine_p], local_sem.at[3]),
    ]
    barrier = pltpu.get_barrier_semaphore()

    near = [me.at(core=1 - me.core)]
    near += [me.at(z=lax.rem(me.z + dz, Z)) for dz in (1, 2, Z - 2, Z - 1)]
    near += [me.at(x=lax.rem(me.x + d, X)) for d in range(1, X)]
    near += [me.at(y=lax.rem(me.y + d, Y)) for d in range(1, Y)]
    for device in near:
        pl.semaphore_signal(barrier, inc=1, device_id=device, device_id_type=MESH)
    for copy in own:
        copy.start()
    pl.semaphore_wait(barrier, len(near))

    teacher_in = Gather(me, tt_hbm, ti_hbm, tt, it, gather_sem.at[0], line_r.at[0], plane_r.at[0], other_r.at[0])
    student_in = Gather(me, st_hbm, si_hbm, st, is_, gather_sem.at[1], line_r.at[1], plane_r.at[1], other_r.at[1])
    student_in.line_near()
    teacher_in.line_far()
    student_in.plane_begin()
    teacher_in.plane_begin()
    student_in.plane_rest()
    teacher_in.plane_rest()
    student_in.line_next()
    teacher_in.line_near()
    student_in.plane_turn()
    teacher_in.plane_turn()
    student_in.line_turn(False)
    student_in.line_last(False)
    teacher_in.line_turn(True)
    teacher_in.line_last(True)
    teacher_in.line_share()
    for copy in own:
        copy.wait()

    def tiles_of(k, texts_buf, image_buf):
        width = texts_buf.shape[2]
        scale = math.log2(math.e) / math.sqrt(width)
        block = texts_buf[pl.ds(k * cut, cut)].reshape(CHUNK, width)
        return [dot(block, image_buf[pl.ds(a * 8, 8)].reshape(width, 256), 1, 0) * scale for a in range(images // 256)]

    def stats(k, which, tiles, er, ec, seen):
        rows = pl.ds(pl.multiple_of(k * CHUNK, CHUNK), CHUNK)
        top = jnp.max(functools.reduce(jnp.maximum, tiles), axis=1, keepdims=True)
        col_max[which, rows] = top
        sums = []
        for a, tile in enumerate(tiles):
            cols = pl.ds(a * 256, 256)
            e_col = jnp.exp2(tile - top)
            ec[rows, cols] = e_col
            sums.append(e_col)
            high = jnp.max(tile, axis=0, keepdims=True)
            e_row = jnp.exp2(tile - high)
            er[rows, cols] = e_row
            row_max[which, pl.ds(k, 1), cols] = high
            row_sum[which, pl.ds(k, 1), cols] = jnp.sum(e_row, axis=0, keepdims=True)
            seen(rows, cols, tile, e_row, e_col)
        total = jnp.sum(functools.reduce(jnp.add, sums), axis=1, keepdims=True)
        return top + jnp.log2(total), total

    def row_stats(which):
        high = row_max[which]
        top = jnp.max(high, axis=0, keepdims=True)
        part = jnp.exp2(high - top)
        total = jnp.sum(row_sum[which] * part, axis=0, keepdims=True)
        return top + jnp.log2(total), part, total

    def lay(ref, first, lanes):
        for a in range(4):
            ref[first + a : first + a + 1, :] = lanes[:, a * 128 : a * 128 + 128]

    planes = sorted(((dx, dy) for dx in range(X) for dy in range(Y) if dx or dy), key=lambda o: -far(o[0], X) - far(o[1], Y))
    lines = sorted(((dz, dc) for dz in range(Z) for dc in range(2) if dz or dc), key=lambda o: -far(o[0], Z))
    groups = ((s_plane, gs_plane), (t_plane, gt_plane), (k_plane, gk_plane)), (
        (s_line, gs_line), (t_line, gt_line), (k_line, gk_line))

    def tell_plane(n):
        msg, got = groups[0][n]
        for dx, dy in planes:
            to = me.at(x=lax.rem(me.x + dx, X), y=lax.rem(me.y + dy, Y))
            send(msg, got.at[dy * X + dx], small_s.at[n, 0], small_r.at[n, 0], to)

    def tell_line(n):
        msg, got = groups[1][n]
        for dz, dc in lines:
            to = me.at(z=lax.rem(me.z + dz, Z), core=lax.rem(me.core + dc, 2))
            send(msg, got.at[dc * Z + dz], small_s.at[n, 1], small_r.at[n, 1], to)

    def hear(n, g):
        msg, got = groups[g][n]
        got[0] = msg[...]
        wait_for(got.at[pl.ds(1, 15)], small_r.at[n, g])
        every = got[...]
        top = jnp.max(every, axis=0)
        return top + jnp.log2(jnp.sum(jnp.exp2(every - top[None]), axis=0))

    def by_core(source, step):
        per_core = chunks // 2
        for core in (me.core, 1 - me.core):
            for k in range(per_core):
                step(core * per_core + k)
            if core is me.core:
                source.other_finish()

    student_in.line_finish()
    student_in.plane_finish()
    if stage >= 2:

        def student_chunk(k):
            tiles = tiles_of(k, st, is_)

            def seen(rows, cols, tile, e_row, e_col):
                s2[rows, cols] = tile

            lse, _ = stats(k, 1, tiles, ers, ecs, seen)
            s_line[pl.ds(k, 1), :] = to_lanes(lse)

        by_core(student_in, student_chunk)
        if stage >= 3:
            tell_line(0)
        lay(s_plane, 0, row_stats(1)[0])
        if stage >= 3:
            tell_plane(0)
    teacher_in.line_finish()
    teacher_in.plane_finish()
    if stage >= 2:

        def teacher_chunk(k):
            tiles = tiles_of(k, tt, it)

            def seen(rows, cols, tile, e_row, e_col):
                t2[rows, cols] = tile

            lse, total = stats(k, 0, tiles, ert, ect, seen)
            col_sum[pl.ds(pl.multiple_of(k * CHUNK, CHUNK), CHUNK)] = total
            t_line[pl.ds(k, 1), :] = to_lanes(lse)

        by_core(teacher_in, teacher_chunk)
        if stage >= 3:
            tell_line(1)
        lse, part, total = row_stats(0)
        lay(t_plane, 0, lse)
    if stage >= 3:
        tell_plane(1)
        row_kl = jnp.zeros((1, images), F32)
        for k in range(chunks):
            rows = pl.ds(k * CHUNK, CHUNK)
            gap = t2[rows, :] - s2[rows, :]
            row_kl += jnp.sum(ert[rows, :] * gap, axis=0, keepdims=True) * part[k : k + 1, :]
            kl = jnp.sum(ect[rows, :] * gap, axis=1, keepdims=True) / col_sum[rows]
            k_line[pl.ds(k, 1), :] = to_lanes(kl)
        lay(k_plane, 0, row_kl / total)
        tell_plane(2)
        tell_line(2)
        lse_s = [hear(0, 0), hear(0, 1)]
        if stage >= 4:
            image_lse = across([lse_s[0][a : a + 1, :] for a in range(4)])
            col_lse[...] = lse_s[1]

            def student_part(k, carry):
                rows = pl.ds(pl.multiple_of(k * CHUNK, CHUNK), CHUNK)
                by_row = jnp.exp2(row_max[1, pl.ds(k, 1), :] - image_lse) * pairs
                by_col = jnp.exp2(col_max[1, rows] - to_rows(col_lse[pl.ds(k, 1), :])) * pairs
                ers[rows, :] = ers[rows, :] * by_row + ecs[rows, :] * by_col
                return carry

            lax.fori_loop(0, chunks, student_part, 0)
        lse_t = [hear(1, 0), hear(1, 1)]

    if stage >= 4:
        image_lse = across([lse_t[0][a : a + 1, :] for a in range(4)])
        col_lse[...] = lse_t[1]
        other = 1 - me.core

        def weigh(k):
            rows = pl.ds(pl.multiple_of(k * CHUNK, CHUNK), CHUNK)
            by_row = jnp.exp2(row_max[0, pl.ds(k, 1), :] - image_lse) * pairs
            by_col = jnp.exp2(col_max[0, rows] - to_rows(col_lse[pl.ds(k, 1), :])) * pairs
            w[rows, :] = (ers[rows, :] - ert[rows, :] * by_row - ect[rows, :] * by_col).astype(BF16)

        def text_part(k):
            rows = pl.ds(pl.multiple_of(k * CHUNK, CHUNK), CHUNK)
            parts = [
                dot(w[rows, pl.ds(a * 256, 256)], is_[pl.ds(a * 8, 8)].reshape(student, 256), 1, 1)
                for a in range(images // 256)
            ]
            return functools.reduce(jnp.add, parts).reshape(cut, ROWS, student)

        per_core = chunks // 2

        def give_line(n):
            part = pl.ds(n * cut, cut)
            wait_for(tsib.at[part], sib_r.at[n])
            tc[part] = (tp[part] + tsib[part].astype(F32)).astype(BF16)
            for z in range(n * cut, (n + 1) * cut):

                @pl.when(me.z != z)
                def _():
                    to = rt.at[lax.rem(z - me.z + Z, Z)]
                    send(tc.at[z], to, grad_s.at[1], grad_r.at[1], me.at(z=z))

        def give_plane(dy):
            y = lax.rem(me.y + dy, Y)
            block = w[:, pl.ds(pl.multiple_of(y * CHUNK, CHUNK), CHUNK)]
            part = dot(block, st[...].reshape(texts, student), 0, 0)
            ip[pl.ds(y * X, X)] = part.astype(BF16).reshape(X, ROWS, student)
            for dx in (2, 1, 3, 0):
                if dx or dy:
                    slot = y * X + lax.rem(me.x + dx, X)

                    @pl.when(jnp.logical_or(slot != 0, me.z != 0))
                    def _():
                        send(ip.at[slot], ri.at[dy * X + dx], grad_s.at[0], grad_r.at[0], me.in_plane(slot))

        def swap(n):
            part = pl.ds(n * cut, cut)
            tsend[part] = text_part(other * per_core + n).astype(BF16)
            send(tsend.at[part], tsib.at[part], sib_s.at[n], sib_r.at[n], me.at(core=other))

        def keep(n):
            tp[pl.ds(n * cut, cut)] = text_part(me.core * per_core + n)

        weigh(other * per_core)
        swap(0)
        weigh(me.core * per_core)
        weigh(other * per_core + 1)
        weigh(me.core * per_core + 1)
        @pl.when(jnp.logical_and(me.z == 0, mine_p != 0))
        def _():
            part = dot(w[:, :CHUNK], st[...].reshape(texts, student), 0, 0)
            ip0[...] = part[:ROWS].astype(BF16)
            to = ri.at[lax.rem(Y - me.y, Y) * X + lax.rem(X - me.x, X)]
            send(ip0, to, grad_s.at[0], grad_r.at[0], me.in_plane(0))

        give_plane(2)
        swap(1)
        keep(0)
        give_plane(1)
        give_line(0)
        give_plane(3)
        keep(1)
        give_plane(0)
        give_line(1)

        for g, (_, (_, got_t), (msg, got)) in enumerate(groups):
            mine = (mine_p, mine_l)[g]
            got[0] = msg[...]
            wait_for(got.at[pl.ds(1, 15)], small_r.at[2, g])
            share = jnp.exp2(got_t[...] - lse_t[g][None])
            loss = jnp.sum(got[...] * share, axis=0) - lse_t[g] + lse_s[g]
            picked = lax.broadcasted_iota(jnp.int32, loss.shape, 0) == lax.div(mine, 4)
            row = jnp.sum(jnp.where(picked, loss, 0.0), axis=0, keepdims=True)
            turned = pltpu.roll(jnp.broadcast_to(row, (8, 128)), lax.rem(128 - lax.rem(mine, 4) * ROWS, 128), 1)
            (row_out, col_out)[g][...] = turned

        ri[0] = ip[mine_p]
        rt[0] = tc[me.z]
        wait_for(ri.at[pl.ds(1, PLANE - 1)], grad_r.at[0])
        image_out[...] = jnp.sum(ri[...].astype(F32), axis=0)
        wait_for(rt.at[pl.ds(1, Z - 1)], grad_r.at[1])
        text_out[...] = jnp.sum(rt[...].astype(F32), axis=0)
        for n in range(2):
            wait_for(tsib.at[pl.ds(0, cut)], sib_s.at[n])
        wait_for(ri.at[pl.ds(1, PLANE - 1)], grad_s.at[0])
        wait_for(rt.at[pl.ds(1, Z - 1)], grad_s.at[1])

    if stage == 1:
        student_in.other_finish()
        teacher_in.other_finish()
    if stage >= 3:
        for g in range(2):
            for n in range(3):
                wait_for(groups[g][n][1].at[pl.ds(1, 15)], small_s.at[n, g])
            if stage == 3:
                wait_for(groups[g][2][1].at[pl.ds(1, 15)], small_r.at[2, g])
    student_in.end()
    teacher_in.end()


def body(teacher_image, teacher_text, student_image, student_text, stage=4):
    teacher, student = teacher_text.shape[1], student_text.shape[1]
    texts, images = LINE * ROWS, PLANE * ROWS
    chunks = texts // CHUNK
    vmem = pltpu.VMEM
    dma = pltpu.SemaphoreType.DMA
    tile = vmem((texts, images), F32)
    grads = vmem((Z, ROWS, student), BF16)
    args = (teacher_image, teacher_text, student_image, student_text)
    image_sum, text_sum, row, col = pl.pallas_call(
        functools.partial(kernel, stage),
        out_shape=(
            jax.ShapeDtypeStruct((ROWS, student), F32),
            jax.ShapeDtypeStruct((ROWS, student), F32),
            jax.ShapeDtypeStruct((8, 128), F32),
            jax.ShapeDtypeStruct((8, 128), F32),
        ),
        in_specs=[pl.BlockSpec(memory_space=pltpu.HBM)] * 4,
        out_specs=(pl.BlockSpec(memory_space=pltpu.VMEM),) * 4,
        scratch_shapes=[
            vmem((LINE, ROWS, teacher), BF16),
            vmem((LINE, ROWS, student), BF16),
            vmem((PLANE,) + teacher_image.shape, BF16),
            vmem((PLANE,) + student_image.shape, BF16),
            tile,
            tile,
            tile,
            tile,
            tile,
            tile,
            vmem((texts, images), BF16),
            vmem((2, texts, 1), F32),
            vmem((texts, 1), F32),
            vmem((2, chunks, images), F32),
            vmem((2, chunks, images), F32),
            *[vmem((4, 128), F32)] * 6,
            *[vmem((16, 4, 128), F32)] * 6,
            vmem((4, 128), F32),
            vmem((Z, ROWS, student), F32),
            grads,
            grads,
            grads,
            vmem((PLANE, ROWS, student), BF16),
            vmem((ROWS, student), BF16),
            grads,
            vmem((PLANE, ROWS, student), BF16),
            dma((4,)),
            dma((2, 2)),
            dma((2, 9)),
            dma((2, 7)),
            dma((2,)),
            dma((3, 2)),
            dma((3, 2)),
            dma((2,)),
            dma((2,)),
            dma((2,)),
            dma((2,)),
        ],
        compiler_params=pltpu.CompilerParams(
            collective_id=0, has_side_effects=True, vmem_limit_bytes=40 * 1024 * 1024
        ),
        name="distill",
    )(*[pltpu.with_memory_space_constraint(a, pltpu.HBM) for a in args])
    scale = 1.0 / math.sqrt(student)
    log2 = math.log(2.0)
    return (image_sum * scale, text_sum * scale, row[0, :ROWS] * log2, col[0, :ROWS] * log2)


def solution(mesh):
    in_specs = (P("grp", "blk"), P(("blk", "grp"), None), P("grp", "blk"), P(("blk", "grp"), None))
    out_specs = (
        P(("blk", "grp"), None),
        P(("blk", "grp"), None),
        P(("blk", "grp")),
        P(("blk", "grp")),
    )
    return jax.shard_map(body, mesh=mesh, in_specs=in_specs, out_specs=out_specs, check_vma=False)
```

```python
import functools
import math

import jax
import jax.numpy as jnp
from jax import lax
from jax.experimental import pallas as pl
from jax.experimental.pallas import tpu as pltpu
from jax.sharding import PartitionSpec as P

MESH = pl.DeviceIdType.MESH
X, Y, Z = 4, 4, 8
PLANE, LINE = X * Y, 2 * Z
ROWS = 32
CHUNK = 128
F32 = jnp.float32
BF16 = jnp.bfloat16


class Place:
    def __init__(self):
        blk = lax.axis_index("blk")
        grp = lax.axis_index("grp")
        self.core = blk % 2
        self.z = (blk // 2) % Z
        self.y = (blk // LINE) * 2 + grp // X
        self.x = grp % X

    def at(self, x=None, y=None, z=None, core=None):
        x = self.x if x is None else x
        y = self.y if y is None else y
        z = self.z if z is None else z
        core = self.core if core is None else core
        return ((y // 2) * LINE + z * 2 + core, (y % 2) * X + x)

    def in_plane(self, slot):
        return self.at(x=slot % X, y=slot // X)

    def in_line(self, slot):
        return self.at(z=slot % Z, core=slot // Z)


def far(by, size):
    return min(by, size - by)


def wait_for(ref, sem):
    pltpu.make_async_copy(ref, ref, sem).wait()


def send(src, dst, send_sem, recv_sem, device):
    pltpu.make_async_remote_copy(
        src_ref=src,
        dst_ref=dst,
        send_sem=send_sem,
        recv_sem=recv_sem,
        device_id=device,
        device_id_type=MESH,
    ).start()


class Gather:
    NEAR = (2, -1, 1)

    def __init__(self, me, own_texts, own_images, texts, images, send_sem, line_r, plane_r, other_r):
        self.me, self.texts, self.images = me, texts, images
        self.own_texts, self.own_images = own_texts, own_images
        self.ss, self.line_r, self.plane_r, self.other = send_sem, line_r, plane_r, other_r

    def text(self, dz):
        me = self.me
        return self.texts.at[me.core * Z + lax.rem(me.z + dz + Z, Z)]

    def image(self, dx, dy):
        me = self.me
        return self.images.at[lax.rem(me.y + dy + Y, Y) * X + lax.rem(me.x + dx + X, X)]

    def up(self, ref, sem, by, src=None):
        me = self.me
        send(ref if src is None else src, ref, self.ss.at[0], self.line_r.at[sem], me.at(z=lax.rem(me.z + by + Z, Z)))

    def share(self, dz, src=None):
        ref = self.text(dz)
        send(ref if src is None else src, ref, self.ss.at[0], self.other, self.me.at(core=1 - self.me.core))

    def over(self, ref, sem, axis, by, src=None):
        me = self.me
        if axis == 0:
            to = me.at(x=lax.rem(me.x + by + X, X))
        else:
            to = me.at(y=lax.rem(me.y + by + Y, Y))
        send(ref if src is None else src, ref, self.ss.at[1], self.plane_r.at[sem], to)

    def part(self, block, axis):
        rows = self.images.shape[1] // 2
        return block.at[pl.ds(axis * rows, rows)]

    def plane_begin(self):
        own = self.image(0, 0)
        for n, by in enumerate((2, 1, -1)):
            for axis in range(2):
                self.over(self.part(own, axis), 3 * axis + n, axis, by, self.part(self.own_images, axis))

    def plane_rest(self):
        own = self.image(0, 0)
        for by in (2, 1, -1):
            for axis in range(2):
                self.over(self.part(own, 1 - axis), 6, axis, by, self.part(self.own_images, 1 - axis))

    def halves(self, block):
        half = ROWS // 2
        return block.at[pl.ds(0, half)], block.at[pl.ds(half, half)]

    def line_far(self):
        first, second = self.halves(self.text(0))
        own_first, own_second = self.halves(self.own_texts)
        self.up(first, 0, 2, own_first)
        self.up(second, 1, -2, own_second)
        self.up(second, 7, 2, own_second)
        self.up(first, 8, -2, own_first)

    def line_near(self):
        own = self.text(0)
        self.up(own, 2, 1, self.own_texts)
        self.up(own, 3, -1, self.own_texts)
        self.share(0, self.own_texts)

    def plane_turn(self):
        for n, by in enumerate(self.NEAR):
            for axis in range(2):
                part = self.part(self.image(by, 0) if axis == 0 else self.image(0, by), axis)
                wait_for(part, self.plane_r.at[3 * axis + n])
                for to in (2, 1, -1):
                    self.over(part, 6, 1 - axis, to)

    def line_next(self):
        a, b = self.text(-1), self.text(1)
        wait_for(a, self.line_r.at[2])
        wait_for(b, self.line_r.at[3])
        self.up(a, 0, 1)
        self.up(b, 1, -1)
        self.share(-1)
        self.share(1)

    def line_turn(self, halves):
        a, b = self.text(-2), self.text(2)
        first, second = self.halves(a)[0], self.halves(b)[1]
        wait_for(first if halves else a, self.line_r.at[0])
        self.up(first, 6, 2)
        wait_for(second if halves else b, self.line_r.at[1])
        self.up(second, 6, -2)

    def line_last(self, halves):
        a, b = self.text(-2), self.text(2)
        if halves:
            wait_for(self.halves(a)[1], self.line_r.at[7])
            wait_for(self.halves(b)[0], self.line_r.at[8])
        self.up(a, 4, 1)
        self.up(b, 5, -1)
        self.share(-2)
        self.share(2)

    def line_share(self):
        wait_for(self.text(-1), self.line_r.at[2])
        wait_for(self.text(1), self.line_r.at[3])
        self.share(-1)
        self.share(1)

    def line_finish(self):
        wait_for(self.text(-3), self.line_r.at[4])
        wait_for(self.text(3), self.line_r.at[5])
        self.share(-3)
        self.share(3)
        wait_for(self.text(4), self.line_r.at[6])
        self.share(4)

    def plane_finish(self):
        wait_for(self.images.at[pl.ds(0, 12)], self.plane_r.at[6])

    def other_finish(self):
        wait_for(self.texts.at[pl.ds((1 - self.me.core) * Z, Z)], self.other)

    def end(self):
        wait_for(self.texts.at[pl.ds(0, 15)], self.ss.at[0])
        wait_for(self.images.at[pl.ds(0, 15)], self.ss.at[1])


def diagonal():
    rows = lax.broadcasted_iota(jnp.int32, (CHUNK, CHUNK), 0)
    cols = lax.broadcasted_iota(jnp.int32, (CHUNK, CHUNK), 1)
    return rows == cols


def to_lanes(column):
    return jnp.sum(jnp.where(diagonal(), column, 0.0), axis=0, keepdims=True)


def to_rows(lanes):
    return jnp.sum(jnp.where(diagonal(), lanes, 0.0), axis=1, keepdims=True)


def dot(a, b, ca, cb):
    return lax.dot_general(a, b, (((ca,), (cb,)), ((), ())), preferred_element_type=F32)


def across(parts):
    return jnp.concatenate(parts, axis=1)


def kernel(
    stage,
    ti_hbm, tt_hbm, si_hbm, st_hbm,
    image_out, text_out, row_out, col_out,
    tt, st, it, is_, s2, t2, ert, ect, ers, ecs, w, col_max, col_sum, row_max, row_sum,
    s_line, s_plane, t_line, t_plane, k_line, k_plane,
    gs_line, gs_plane, gt_line, gt_plane, gk_line, gk_plane, col_lse,
    tp, tsend, tsib, tc, ip, ip0, rt, ri,
    local_sem, gather_sem, line_r, plane_r, other_r,
    small_s, small_r, sib_s, sib_r, grad_s, grad_r,
):
    me = Place()
    texts, images = LINE * ROWS, PLANE * ROWS
    teacher, student = tt.shape[2], st.shape[2]
    pairs = float(images * LINE)
    chunks = texts // CHUNK
    cut = CHUNK // ROWS
    mine_p = me.y * X + me.x
    mine_l = me.core * Z + me.z

    own = [
        pltpu.make_async_copy(tt_hbm, tt.at[mine_l], local_sem.at[0]),
        pltpu.make_async_copy(ti_hbm, it.at[mine_p], local_sem.at[1]),
        pltpu.make_async_copy(st_hbm, st.at[mine_l], local_sem.at[2]),
        pltpu.make_async_copy(si_hbm, is_.at[mine_p], local_sem.at[3]),
    ]
    barrier = pltpu.get_barrier_semaphore()

    near = [me.at(core=1 - me.core)]
    near += [me.at(z=lax.rem(me.z + dz, Z)) for dz in (1, 2, Z - 2, Z - 1)]
    near += [me.at(x=lax.rem(me.x + d, X)) for d in range(1, X)]
    near += [me.at(y=lax.rem(me.y + d, Y)) for d in range(1, Y)]
    for device in near:
        pl.semaphore_signal(barrier, inc=1, device_id=device, device_id_type=MESH)
    for copy in own:
        copy.start()
    pl.semaphore_wait(barrier, len(near))

    teacher_in = Gather(me, tt_hbm, ti_hbm, tt, it, gather_sem.at[0], line_r.at[0], plane_r.at[0], other_r.at[0])
    student_in = Gather(me, st_hbm, si_hbm, st, is_, gather_sem.at[1], line_r.at[1], plane_r.at[1], other_r.at[1])
    student_in.line_near()
    teacher_in.line_far()
    student_in.plane_begin()
    teacher_in.plane_begin()
    teacher_in.plane_rest()
    student_in.plane_rest()
    student_in.line_next()
    teacher_in.line_near()
    student_in.plane_turn()
    teacher_in.plane_turn()
    student_in.line_turn(False)
    student_in.line_last(False)
    teacher_in.line_turn(True)
    teacher_in.line_last(True)
    teacher_in.line_share()
    for copy in own:
        copy.wait()

    def tiles_of(k, texts_buf, image_buf):
        width = texts_buf.shape[2]
        scale = math.log2(math.e) / math.sqrt(width)
        block = texts_buf[pl.ds(k * cut, cut)].reshape(CHUNK, width)
        return [dot(block, image_buf[pl.ds(a * 8, 8)].reshape(width, 256), 1, 0) * scale for a in range(images // 256)]

    def stats(k, which, tiles, er, ec, seen):
        rows = pl.ds(pl.multiple_of(k * CHUNK, CHUNK), CHUNK)
        top = jnp.max(functools.reduce(jnp.maximum, tiles), axis=1, keepdims=True)
        col_max[which, rows] = top
        sums = []
        for a, tile in enumerate(tiles):
            cols = pl.ds(a * 256, 256)
            e_col = jnp.exp2(tile - top)
            ec[rows, cols] = e_col
            sums.append(e_col)
            high = jnp.max(tile, axis=0, keepdims=True)
            e_row = jnp.exp2(tile - high)
            er[rows, cols] = e_row
            row_max[which, pl.ds(k, 1), cols] = high
            row_sum[which, pl.ds(k, 1), cols] = jnp.sum(e_row, axis=0, keepdims=True)
            seen(rows, cols, tile, e_row, e_col)
        total = jnp.sum(functools.reduce(jnp.add, sums), axis=1, keepdims=True)
        return top + jnp.log2(total), total

    def row_stats(which):
        high = row_max[which]
        top = jnp.max(high, axis=0, keepdims=True)
        part = jnp.exp2(high - top)
        total = jnp.sum(row_sum[which] * part, axis=0, keepdims=True)
        return top + jnp.log2(total), part, total

    def lay(ref, first, lanes):
        for a in range(4):
            ref[first + a : first + a + 1, :] = lanes[:, a * 128 : a * 128 + 128]

    planes = sorted(((dx, dy) for dx in range(X) for dy in range(Y) if dx or dy), key=lambda o: -far(o[0], X) - far(o[1], Y))
    lines = sorted(((dz, dc) for dz in range(Z) for dc in range(2) if dz or dc), key=lambda o: -far(o[0], Z))
    groups = ((s_plane, gs_plane), (t_plane, gt_plane), (k_plane, gk_plane)), (
        (s_line, gs_line), (t_line, gt_line), (k_line, gk_line))

    def tell_plane(n):
        msg, got = groups[0][n]
        for dx, dy in planes:
            to = me.at(x=lax.rem(me.x + dx, X), y=lax.rem(me.y + dy, Y))
            send(msg, got.at[dy * X + dx], small_s.at[n, 0], small_r.at[n, 0], to)

    def tell_line(n):
        msg, got = groups[1][n]
        for dz, dc in lines:
            to = me.at(z=lax.rem(me.z + dz, Z), core=lax.rem(me.core + dc, 2))
            send(msg, got.at[dc * Z + dz], small_s.at[n, 1], small_r.at[n, 1], to)

    def hear(n, g):
        msg, got = groups[g][n]
        got[0] = msg[...]
        wait_for(got.at[pl.ds(1, 15)], small_r.at[n, g])
        every = got[...]
        top = jnp.max(every, axis=0)
        return top + jnp.log2(jnp.sum(jnp.exp2(every - top[None]), axis=0))

    def by_core(source, step):
        per_core = chunks // 2
        for core in (me.core, 1 - me.core):
            for k in range(per_core):
                step(core * per_core + k)
            if core is me.core:
                source.other_finish()

    student_in.line_finish()
    student_in.plane_finish()
    if stage >= 2:

        def student_chunk(k):
            tiles = tiles_of(k, st, is_)

            def seen(rows, cols, tile, e_row, e_col):
                s2[rows, cols] = tile

            lse, _ = stats(k, 1, tiles, ers, ecs, seen)
            s_line[pl.ds(k, 1), :] = to_lanes(lse)

        by_core(student_in, student_chunk)
        if stage >= 3:
            tell_line(0)
        lay(s_plane, 0, row_stats(1)[0])
        if stage >= 3:
            tell_plane(0)
    teacher_in.line_finish()
    teacher_in.plane_finish()
    if stage >= 2:

        def teacher_chunk(k):
            tiles = tiles_of(k, tt, it)

            def seen(rows, cols, tile, e_row, e_col):
                t2[rows, cols] = tile

            lse, total = stats(k, 0, tiles, ert, ect, seen)
            col_sum[pl.ds(pl.multiple_of(k * CHUNK, CHUNK), CHUNK)] = total
            t_line[pl.ds(k, 1), :] = to_lanes(lse)

        by_core(teacher_in, teacher_chunk)
        if stage >= 3:
            tell_line(1)
        lse, part, total = row_stats(0)
        lay(t_plane, 0, lse)
    if stage >= 3:
        tell_plane(1)
        row_kl = jnp.zeros((1, images), F32)
        for k in range(chunks):
            rows = pl.ds(k * CHUNK, CHUNK)
            gap = t2[rows, :] - s2[rows, :]
            row_kl += jnp.sum(ert[rows, :] * gap, axis=0, keepdims=True) * part[k : k + 1, :]
            kl = jnp.sum(ect[rows, :] * gap, axis=1, keepdims=True) / col_sum[rows]
            k_line[pl.ds(k, 1), :] = to_lanes(kl)
        lay(k_plane, 0, row_kl / total)
        tell_plane(2)
        tell_line(2)
        lse_s = [hear(0, 0), hear(0, 1)]
        if stage >= 4:
            image_lse = across([lse_s[0][a : a + 1, :] for a in range(4)])
            col_lse[...] = lse_s[1]

            def student_part(k, carry):
                rows = pl.ds(pl.multiple_of(k * CHUNK, CHUNK), CHUNK)
                by_row = jnp.exp2(row_max[1, pl.ds(k, 1), :] - image_lse) * pairs
                by_col = jnp.exp2(col_max[1, rows] - to_rows(col_lse[pl.ds(k, 1), :])) * pairs
                ers[rows, :] = ers[rows, :] * by_row + ecs[rows, :] * by_col
                return carry

            lax.fori_loop(0, chunks, student_part, 0)
        lse_t = [hear(1, 0), hear(1, 1)]

    if stage >= 4:
        image_lse = across([lse_t[0][a : a + 1, :] for a in range(4)])
        col_lse[...] = lse_t[1]
        other = 1 - me.core

        def weigh(k):
            rows = pl.ds(pl.multiple_of(k * CHUNK, CHUNK), CHUNK)
            by_row = jnp.exp2(row_max[0, pl.ds(k, 1), :] - image_lse) * pairs
            by_col = jnp.exp2(col_max[0, rows] - to_rows(col_lse[pl.ds(k, 1), :])) * pairs
            w[rows, :] = (ers[rows, :] - ert[rows, :] * by_row - ect[rows, :] * by_col).astype(BF16)

        def text_part(k):
            rows = pl.ds(pl.multiple_of(k * CHUNK, CHUNK), CHUNK)
            parts = [
                dot(w[rows, pl.ds(a * 256, 256)], is_[pl.ds(a * 8, 8)].reshape(student, 256), 1, 1)
                for a in range(images // 256)
            ]
            return functools.reduce(jnp.add, parts).reshape(cut, ROWS, student)

        per_core = chunks // 2

        def give_line(n):
            part = pl.ds(n * cut, cut)
            wait_for(tsib.at[part], sib_r.at[n])
            tc[part] = (tp[part] + tsib[part].astype(F32)).astype(BF16)
            for z in range(n * cut, (n + 1) * cut):

                @pl.when(me.z != z)
                def _():
                    to = rt.at[lax.rem(z - me.z + Z, Z)]
                    send(tc.at[z], to, grad_s.at[1], grad_r.at[1], me.at(z=z))

        def give_plane(dy):
            y = lax.rem(me.y + dy, Y)
            block = w[:, pl.ds(pl.multiple_of(y * CHUNK, CHUNK), CHUNK)]
            part = dot(block, st[...].reshape(texts, student), 0, 0)
            ip[pl.ds(y * X, X)] = part.astype(BF16).reshape(X, ROWS, student)
            for dx in (2, 1, 3, 0):
                if dx or dy:
                    slot = y * X + lax.rem(me.x + dx, X)

                    @pl.when(jnp.logical_or(slot != 0, me.z != 0))
                    def _():
                        send(ip.at[slot], ri.at[dy * X + dx], grad_s.at[0], grad_r.at[0], me.in_plane(slot))

        def swap(n):
            part = pl.ds(n * cut, cut)
            tsend[part] = text_part(other * per_core + n).astype(BF16)
            send(tsend.at[part], tsib.at[part], sib_s.at[n], sib_r.at[n], me.at(core=other))

        def keep(n):
            tp[pl.ds(n * cut, cut)] = text_part(me.core * per_core + n)

        weigh(other * per_core)
        swap(0)
        weigh(me.core * per_core)
        weigh(other * per_core + 1)
        weigh(me.core * per_core + 1)
        @pl.when(jnp.logical_and(me.z == 0, mine_p != 0))
        def _():
            part = dot(w[:, :CHUNK], st[...].reshape(texts, student), 0, 0)
            ip0[...] = part[:ROWS].astype(BF16)
            to = ri.at[lax.rem(Y - me.y, Y) * X + lax.rem(X - me.x, X)]
            send(ip0, to, grad_s.at[0], grad_r.at[0], me.in_plane(0))

        give_plane(2)
        swap(1)
        keep(0)
        give_plane(1)
        give_line(0)
        give_plane(3)
        keep(1)
        give_plane(0)
        give_line(1)

        for g, (_, (_, got_t), (msg, got)) in enumerate(groups):
            mine = (mine_p, mine_l)[g]
            got[0] = msg[...]
            wait_for(got.at[pl.ds(1, 15)], small_r.at[2, g])
            share = jnp.exp2(got_t[...] - lse_t[g][None])
            loss = jnp.sum(got[...] * share, axis=0) - lse_t[g] + lse_s[g]
            picked = lax.broadcasted_iota(jnp.int32, loss.shape, 0) == lax.div(mine, 4)
            row = jnp.sum(jnp.where(picked, loss, 0.0), axis=0, keepdims=True)
            turned = pltpu.roll(jnp.broadcast_to(row, (8, 128)), lax.rem(128 - lax.rem(mine, 4) * ROWS, 128), 1)
            (row_out, col_out)[g][...] = turned

        ri[0] = ip[mine_p]
        rt[0] = tc[me.z]
        wait_for(ri.at[pl.ds(1, PLANE - 1)], grad_r.at[0])
        image_out[...] = jnp.sum(ri[...].astype(F32), axis=0)
        wait_for(rt.at[pl.ds(1, Z - 1)], grad_r.at[1])
        text_out[...] = jnp.sum(rt[...].astype(F32), axis=0)
        for n in range(2):
            wait_for(tsib.at[pl.ds(0, cut)], sib_s.at[n])
        wait_for(ri.at[pl.ds(1, PLANE - 1)], grad_s.at[0])
        wait_for(rt.at[pl.ds(1, Z - 1)], grad_s.at[1])

    if stage == 1:
        student_in.other_finish()
        teacher_in.other_finish()
    if stage >= 3:
        for g in range(2):
            for n in range(3):
                wait_for(groups[g][n][1].at[pl.ds(1, 15)], small_s.at[n, g])
            if stage == 3:
                wait_for(groups[g][2][1].at[pl.ds(1, 15)], small_r.at[2, g])
    student_in.end()
    teacher_in.end()


def body(teacher_image, teacher_text, student_image, student_text, stage=4):
    teacher, student = teacher_text.shape[1], student_text.shape[1]
    texts, images = LINE * ROWS, PLANE * ROWS
    chunks = texts // CHUNK
    vmem = pltpu.VMEM
    dma = pltpu.SemaphoreType.DMA
    tile = vmem((texts, images), F32)
    grads = vmem((Z, ROWS, student), BF16)
    args = (teacher_image, teacher_text, student_image, student_text)
    image_sum, text_sum, row, col = pl.pallas_call(
        functools.partial(kernel, stage),
        out_shape=(
            jax.ShapeDtypeStruct((ROWS, student), F32),
            jax.ShapeDtypeStruct((ROWS, student), F32),
            jax.ShapeDtypeStruct((8, 128), F32),
            jax.ShapeDtypeStruct((8, 128), F32),
        ),
        in_specs=[pl.BlockSpec(memory_space=pltpu.HBM)] * 4,
        out_specs=(pl.BlockSpec(memory_space=pltpu.VMEM),) * 4,
        scratch_shapes=[
            vmem((LINE, ROWS, teacher), BF16),
            vmem((LINE, ROWS, student), BF16),
            vmem((PLANE,) + teacher_image.shape, BF16),
            vmem((PLANE,) + student_image.shape, BF16),
            tile,
            tile,
            tile,
            tile,
            tile,
            tile,
            vmem((texts, images), BF16),
            vmem((2, texts, 1), F32),
            vmem((texts, 1), F32),
            vmem((2, chunks, images), F32),
            vmem((2, chunks, images), F32),
            *[vmem((4, 128), F32)] * 6,
            *[vmem((16, 4, 128), F32)] * 6,
            vmem((4, 128), F32),
            vmem((Z, ROWS, student), F32),
            grads,
            grads,
            grads,
            vmem((PLANE, ROWS, student), BF16),
            vmem((ROWS, student), BF16),
            grads,
            vmem((PLANE, ROWS, student), BF16),
            dma((4,)),
            dma((2, 2)),
            dma((2, 9)),
            dma((2, 7)),
            dma((2,)),
            dma((3, 2)),
            dma((3, 2)),
            dma((2,)),
            dma((2,)),
            dma((2,)),
            dma((2,)),
        ],
        compiler_params=pltpu.CompilerParams(
            collective_id=0, has_side_effects=True, vmem_limit_bytes=40 * 1024 * 1024
        ),
        name="distill",
    )(*[pltpu.with_memory_space_constraint(a, pltpu.HBM) for a in args])
    scale = 1.0 / math.sqrt(student)
    log2 = math.log(2.0)
    return (image_sum * scale, text_sum * scale, row[0, :ROWS] * log2, col[0, :ROWS] * log2)


def solution(mesh):
    in_specs = (P("grp", "blk"), P(("blk", "grp"), None), P("grp", "blk"), P(("blk", "grp"), None))
    out_specs = (
        P(("blk", "grp"), None),
        P(("blk", "grp"), None),
        P(("blk", "grp")),
        P(("blk", "grp")),
    )
    return jax.shard_map(body, mesh=mesh, in_specs=in_specs, out_specs=out_specs, check_vma=False)
```

```python
import functools
import math

import jax
import jax.numpy as jnp
from jax import lax
from jax.experimental import pallas as pl
from jax.experimental.pallas import tpu as pltpu
from jax.sharding import PartitionSpec as P

MESH = pl.DeviceIdType.MESH
X, Y, Z = 4, 4, 8
PLANE, LINE = X * Y, 2 * Z
ROWS = 32
CHUNK = 128
F32 = jnp.float32
BF16 = jnp.bfloat16


class Place:
    def __init__(self):
        blk = lax.axis_index("blk")
        grp = lax.axis_index("grp")
        self.core = blk % 2
        self.z = (blk // 2) % Z
        self.y = (blk // LINE) * 2 + grp // X
        self.x = grp % X

    def at(self, x=None, y=None, z=None, core=None):
        x = self.x if x is None else x
        y = self.y if y is None else y
        z = self.z if z is None else z
        core = self.core if core is None else core
        return ((y // 2) * LINE + z * 2 + core, (y % 2) * X + x)

    def in_plane(self, slot):
        return self.at(x=slot % X, y=slot // X)

    def in_line(self, slot):
        return self.at(z=slot % Z, core=slot // Z)


def far(by, size):
    return min(by, size - by)


def wait_for(ref, sem):
    pltpu.make_async_copy(ref, ref, sem).wait()


def send(src, dst, send_sem, recv_sem, device):
    pltpu.make_async_remote_copy(
        src_ref=src,
        dst_ref=dst,
        send_sem=send_sem,
        recv_sem=recv_sem,
        device_id=device,
        device_id_type=MESH,
    ).start()


class Gather:
    NEAR = (2, -1, 1)

    def __init__(self, me, own_texts, own_images, texts, images, send_sem, line_r, plane_r, other_r):
        self.me, self.texts, self.images = me, texts, images
        self.own_texts, self.own_images = own_texts, own_images
        self.ss, self.line_r, self.plane_r, self.other = send_sem, line_r, plane_r, other_r

    def text(self, dz):
        me = self.me
        return self.texts.at[me.core * Z + lax.rem(me.z + dz + Z, Z)]

    def image(self, dx, dy):
        me = self.me
        return self.images.at[lax.rem(me.y + dy + Y, Y) * X + lax.rem(me.x + dx + X, X)]

    def up(self, ref, sem, by, src=None):
        me = self.me
        send(ref if src is None else src, ref, self.ss.at[0], self.line_r.at[sem], me.at(z=lax.rem(me.z + by + Z, Z)))

    def share(self, dz, src=None):
        ref = self.text(dz)
        send(ref if src is None else src, ref, self.ss.at[0], self.other, self.me.at(core=1 - self.me.core))

    def over(self, ref, sem, axis, by, src=None):
        me = self.me
        if axis == 0:
            to = me.at(x=lax.rem(me.x + by + X, X))
        else:
            to = me.at(y=lax.rem(me.y + by + Y, Y))
        send(ref if src is None else src, ref, self.ss.at[1], self.plane_r.at[sem], to)

    def part(self, block, axis):
        rows = self.images.shape[1] // 2
        return block.at[pl.ds(axis * rows, rows)]

    def plane_begin(self):
        own = self.image(0, 0)
        for n, by in enumerate((2, 1, -1)):
            for axis in range(2):
                self.over(self.part(own, axis), 3 * axis + n, axis, by, self.part(self.own_images, axis))

    def plane_rest(self):
        own = self.image(0, 0)
        for by in (2, 1, -1):
            for axis in range(2):
                self.over(self.part(own, 1 - axis), 6, axis, by, self.part(self.own_images, 1 - axis))

    def halves(self, block):
        half = ROWS // 2
        return block.at[pl.ds(0, half)], block.at[pl.ds(half, half)]

    def line_far(self):
        first, second = self.halves(self.text(0))
        own_first, own_second = self.halves(self.own_texts)
        self.up(first, 0, 2, own_first)
        self.up(second, 1, -2, own_second)
        self.up(second, 7, 2, own_second)
        self.up(first, 8, -2, own_first)

    def line_near(self):
        own = self.text(0)
        self.up(own, 2, 1, self.own_texts)
        self.up(own, 3, -1, self.own_texts)
        self.share(0, self.own_texts)

    def plane_turn(self):
        for n, by in enumerate(self.NEAR):
            for axis in range(2):
                part = self.part(self.image(by, 0) if axis == 0 else self.image(0, by), axis)
                wait_for(part, self.plane_r.at[3 * axis + n])
                for to in (2, 1, -1):
                    self.over(part, 6, 1 - axis, to)

    def line_next(self):
        a, b = self.text(-1), self.text(1)
        wait_for(a, self.line_r.at[2])
        wait_for(b, self.line_r.at[3])
        self.up(a, 0, 1)
        self.up(b, 1, -1)
        self.share(-1)
        self.share(1)

    def line_turn(self, halves):
        a, b = self.text(-2), self.text(2)
        first, second = self.halves(a)[0], self.halves(b)[1]
        wait_for(first if halves else a, self.line_r.at[0])
        self.up(first, 6, 2)
        wait_for(second if halves else b, self.line_r.at[1])
        self.up(second, 6, -2)

    def line_last(self, halves):
        a, b = self.text(-2), self.text(2)
        if halves:
            wait_for(self.halves(a)[1], self.line_r.at[7])
            wait_for(self.halves(b)[0], self.line_r.at[8])
        self.up(a, 4, 1)
        self.up(b, 5, -1)
        self.share(-2)
        self.share(2)

    def line_share(self):
        wait_for(self.text(-1), self.line_r.at[2])
        wait_for(self.text(1), self.line_r.at[3])
        self.share(-1)
        self.share(1)

    def line_finish(self):
        wait_for(self.text(-3), self.line_r.at[4])
        wait_for(self.text(3), self.line_r.at[5])
        self.share(-3)
        self.share(3)
        wait_for(self.text(4), self.line_r.at[6])
        self.share(4)

    def plane_finish(self):
        wait_for(self.images.at[pl.ds(0, 12)], self.plane_r.at[6])

    def other_finish(self):
        wait_for(self.texts.at[pl.ds((1 - self.me.core) * Z, Z)], self.other)

    def end(self):
        wait_for(self.texts.at[pl.ds(0, 15)], self.ss.at[0])
        wait_for(self.images.at[pl.ds(0, 15)], self.ss.at[1])


def diagonal():
    rows = lax.broadcasted_iota(jnp.int32, (CHUNK, CHUNK), 0)
    cols = lax.broadcasted_iota(jnp.int32, (CHUNK, CHUNK), 1)
    return rows == cols


def to_lanes(column):
    return jnp.sum(jnp.where(diagonal(), column, 0.0), axis=0, keepdims=True)


def to_rows(lanes):
    return jnp.sum(jnp.where(diagonal(), lanes, 0.0), axis=1, keepdims=True)


def dot(a, b, ca, cb):
    return lax.dot_general(a, b, (((ca,), (cb,)), ((), ())), preferred_element_type=F32)


def across(parts):
    return jnp.concatenate(parts, axis=1)


def kernel(
    stage,
    ti_hbm, tt_hbm, si_hbm, st_hbm,
    image_out, text_out, row_out, col_out,
    tt, st, it, is_, s2, t2, ert, ect, ers, ecs, w, col_max, col_sum, row_max, row_sum,
    s_line, s_plane, t_line, t_plane, k_line, k_plane,
    gs_line, gs_plane, gt_line, gt_plane, gk_line, gk_plane, col_lse,
    tp, tsend, tsib, tc, ip, ip0, rt, ri,
    local_sem, gather_sem, line_r, plane_r, other_r,
    small_s, small_r, sib_s, sib_r, grad_s, grad_r,
):
    me = Place()
    texts, images = LINE * ROWS, PLANE * ROWS
    teacher, student = tt.shape[2], st.shape[2]
    pairs = float(images * LINE)
    chunks = texts // CHUNK
    cut = CHUNK // ROWS
    mine_p = me.y * X + me.x
    mine_l = me.core * Z + me.z

    own = [
        pltpu.make_async_copy(tt_hbm, tt.at[mine_l], local_sem.at[0]),
        pltpu.make_async_copy(ti_hbm, it.at[mine_p], local_sem.at[1]),
        pltpu.make_async_copy(st_hbm, st.at[mine_l], local_sem.at[2]),
        pltpu.make_async_copy(si_hbm, is_.at[mine_p], local_sem.at[3]),
    ]
    barrier = pltpu.get_barrier_semaphore()

    near = [me.at(core=1 - me.core)]
    near += [me.at(z=lax.rem(me.z + dz, Z)) for dz in (1, 2, Z - 2, Z - 1)]
    near += [me.at(x=lax.rem(me.x + d, X)) for d in range(1, X)]
    near += [me.at(y=lax.rem(me.y + d, Y)) for d in range(1, Y)]
    for device in near:
        pl.semaphore_signal(barrier, inc=1, device_id=device, device_id_type=MESH)
    for copy in own:
        copy.start()
    pl.semaphore_wait(barrier, len(near))

    teacher_in = Gather(me, tt_hbm, ti_hbm, tt, it, gather_sem.at[0], line_r.at[0], plane_r.at[0], other_r.at[0])
    student_in = Gather(me, st_hbm, si_hbm, st, is_, gather_sem.at[1], line_r.at[1], plane_r.at[1], other_r.at[1])
    student_in.line_near()
    teacher_in.line_far()
    student_in.plane_begin()
    teacher_in.plane_begin()
    student_in.plane_rest()
    teacher_in.plane_rest()
    student_in.line_next()
    teacher_in.line_near()
    student_in.plane_turn()
    teacher_in.plane_turn()
    student_in.line_turn(False)
    student_in.line_last(False)
    teacher_in.line_turn(True)
    teacher_in.line_last(True)
    teacher_in.line_share()
    for copy in own:
        copy.wait()

    def tiles_of(k, texts_buf, image_buf):
        width = texts_buf.shape[2]
        scale = math.log2(math.e) / math.sqrt(width)
        block = texts_buf[pl.ds(k * cut, cut)].reshape(CHUNK, width)
        return [dot(block, image_buf[pl.ds(a * 8, 8)].reshape(width, 256), 1, 0) * scale for a in range(images // 256)]

    def stats(k, which, tiles, er, ec, seen):
        rows = pl.ds(pl.multiple_of(k * CHUNK, CHUNK), CHUNK)
        top = jnp.max(functools.reduce(jnp.maximum, tiles), axis=1, keepdims=True)
        col_max[which, rows] = top
        sums = []
        for a, tile in enumerate(tiles):
            cols = pl.ds(a * 256, 256)
            e_col = jnp.exp2(tile - top)
            ec[rows, cols] = e_col
            sums.append(e_col)
            high = jnp.max(tile, axis=0, keepdims=True)
            e_row = jnp.exp2(tile - high)
            er[rows, cols] = e_row
            row_max[which, pl.ds(k, 1), cols] = high
            row_sum[which, pl.ds(k, 1), cols] = jnp.sum(e_row, axis=0, keepdims=True)
            seen(rows, cols, tile, e_row, e_col)
        total = jnp.sum(functools.reduce(jnp.add, sums), axis=1, keepdims=True)
        return top + jnp.log2(total), total

    def row_stats(which):
        high = row_max[which]
        top = jnp.max(high, axis=0, keepdims=True)
        part = jnp.exp2(high - top)
        total = jnp.sum(row_sum[which] * part, axis=0, keepdims=True)
        return top + jnp.log2(total), part, total

    def lay(ref, first, lanes):
        for a in range(4):
            ref[first + a : first + a + 1, :] = lanes[:, a * 128 : a * 128 + 128]

    planes = sorted(((dx, dy) for dx in range(X) for dy in range(Y) if dx or dy), key=lambda o: -far(o[0], X) - far(o[1], Y))
    lines = sorted(((dz, dc) for dz in range(Z) for dc in range(2) if dz or dc), key=lambda o: -far(o[0], Z))
    groups = ((s_plane, gs_plane), (t_plane, gt_plane), (k_plane, gk_plane)), (
        (s_line, gs_line), (t_line, gt_line), (k_line, gk_line))

    def tell_plane(n):
        msg, got = groups[0][n]
        for dx, dy in planes:
            to = me.at(x=lax.rem(me.x + dx, X), y=lax.rem(me.y + dy, Y))
            send(msg, got.at[dy * X + dx], small_s.at[n, 0], small_r.at[n, 0], to)

    def tell_line(n):
        msg, got = groups[1][n]
        for dz, dc in lines:
            to = me.at(z=lax.rem(me.z + dz, Z), core=lax.rem(me.core + dc, 2))
            send(msg, got.at[dc * Z + dz], small_s.at[n, 1], small_r.at[n, 1], to)

    def hear(n, g):
        msg, got = groups[g][n]
        got[0] = msg[...]
        wait_for(got.at[pl.ds(1, 15)], small_r.at[n, g])
        every = got[...]
        top = jnp.max(every, axis=0)
        return top + jnp.log2(jnp.sum(jnp.exp2(every - top[None]), axis=0))

    def by_core(source, step):
        per_core = chunks // 2
        for core in (me.core, 1 - me.core):
            for k in range(per_core):
                step(core * per_core + k)
            if core is me.core:
                source.other_finish()

    student_in.line_finish()
    student_in.plane_finish()
    if stage >= 2:

        def student_chunk(k):
            tiles = tiles_of(k, st, is_)

            def seen(rows, cols, tile, e_row, e_col):
                s2[rows, cols] = tile

            lse, _ = stats(k, 1, tiles, ers, ecs, seen)
            s_line[pl.ds(k, 1), :] = to_lanes(lse)

        by_core(student_in, student_chunk)
        if stage >= 3:
            tell_line(0)
        lay(s_plane, 0, row_stats(1)[0])
        if stage >= 3:
            tell_plane(0)
    teacher_in.line_finish()
    teacher_in.plane_finish()
    if stage >= 2:

        def teacher_chunk(k):
            tiles = tiles_of(k, tt, it)

            def seen(rows, cols, tile, e_row, e_col):
                t2[rows, cols] = tile

            lse, total = stats(k, 0, tiles, ert, ect, seen)
            col_sum[pl.ds(pl.multiple_of(k * CHUNK, CHUNK), CHUNK)] = total
            t_line[pl.ds(k, 1), :] = to_lanes(lse)

        by_core(teacher_in, teacher_chunk)
        if stage >= 3:
            tell_line(1)
        lse, part, total = row_stats(0)
        lay(t_plane, 0, lse)
    if stage >= 3:
        tell_plane(1)
        row_kl = jnp.zeros((1, images), F32)
        for k in range(chunks):
            rows = pl.ds(k * CHUNK, CHUNK)
            gap = t2[rows, :] - s2[rows, :]
            row_kl += jnp.sum(ert[rows, :] * gap, axis=0, keepdims=True) * part[k : k + 1, :]
            kl = jnp.sum(ect[rows, :] * gap, axis=1, keepdims=True) / col_sum[rows]
            k_line[pl.ds(k, 1), :] = to_lanes(kl)
        lay(k_plane, 0, row_kl / total)
        tell_plane(2)
        tell_line(2)
        lse_s = [hear(0, 0), hear(0, 1)]
        if stage >= 4:
            image_lse = across([lse_s[0][a : a + 1, :] for a in range(4)])
            col_lse[...] = lse_s[1]

            def student_part(k, carry):
                rows = pl.ds(pl.multiple_of(k * CHUNK, CHUNK), CHUNK)
                by_row = jnp.exp2(row_max[1, pl.ds(k, 1), :] - image_lse) * pairs
                by_col = jnp.exp2(col_max[1, rows] - to_rows(col_lse[pl.ds(k, 1), :])) * pairs
                ers[rows, :] = ers[rows, :] * by_row + ecs[rows, :] * by_col
                return carry

            lax.fori_loop(0, chunks, student_part, 0)
        lse_t = [hear(1, 0), hear(1, 1)]

    if stage >= 4:
        image_lse = across([lse_t[0][a : a + 1, :] for a in range(4)])
        col_lse[...] = lse_t[1]
        other = 1 - me.core

        def weigh(k):
            rows = pl.ds(pl.multiple_of(k * CHUNK, CHUNK), CHUNK)
            by_row = jnp.exp2(row_max[0, pl.ds(k, 1), :] - image_lse) * pairs
            by_col = jnp.exp2(col_max[0, rows] - to_rows(col_lse[pl.ds(k, 1), :])) * pairs
            w[rows, :] = (ers[rows, :] - ert[rows, :] * by_row - ect[rows, :] * by_col).astype(BF16)

        def text_part(k):
            rows = pl.ds(pl.multiple_of(k * CHUNK, CHUNK), CHUNK)
            parts = [
                dot(w[rows, pl.ds(a * 256, 256)], is_[pl.ds(a * 8, 8)].reshape(student, 256), 1, 1)
                for a in range(images // 256)
            ]
            return functools.reduce(jnp.add, parts).reshape(cut, ROWS, student)

        per_core = chunks // 2

        def give_line(n):
            part = pl.ds(n * cut, cut)
            wait_for(tsib.at[part], sib_r.at[n])
            tc[part] = (tp[part] + tsib[part].astype(F32)).astype(BF16)
            for z in range(n * cut, (n + 1) * cut):

                @pl.when(me.z != z)
                def _():
                    to = rt.at[lax.rem(z - me.z + Z, Z)]
                    send(tc.at[z], to, grad_s.at[1], grad_r.at[1], me.at(z=z))

        def give_plane(dy):
            y = lax.rem(me.y + dy, Y)
            block = w[:, pl.ds(pl.multiple_of(y * CHUNK, CHUNK), CHUNK)]
            part = dot(block, st[...].reshape(texts, student), 0, 0)
            ip[pl.ds(y * X, X)] = part.astype(BF16).reshape(X, ROWS, student)
            for dx in (2, 1, 3, 0):
                if dx or dy:
                    slot = y * X + lax.rem(me.x + dx, X)

                    @pl.when(jnp.logical_or(slot != 0, me.z != 0))
                    def _():
                        send(ip.at[slot], ri.at[dy * X + dx], grad_s.at[0], grad_r.at[0], me.in_plane(slot))

        def swap(n):
            part = pl.ds(n * cut, cut)
            tsend[part] = text_part(other * per_core + n).astype(BF16)
            send(tsend.at[part], tsib.at[part], sib_s.at[n], sib_r.at[n], me.at(core=other))

        def keep(n):
            tp[pl.ds(n * cut, cut)] = text_part(me.core * per_core + n)

        weigh(other * per_core)
        swap(0)
        weigh(me.core * per_core)
        weigh(other * per_core + 1)
        weigh(me.core * per_core + 1)
        @pl.when(jnp.logical_and(me.z == 0, mine_p != 0))
        def _():
            part = dot(w[:, :CHUNK], st[...].reshape(texts, student), 0, 0)
            ip0[...] = part[:ROWS].astype(BF16)
            to = ri.at[lax.rem(Y - me.y, Y) * X + lax.rem(X - me.x, X)]
            send(ip0, to, grad_s.at[0], grad_r.at[0], me.in_plane(0))

        give_plane(2)
        swap(1)
        keep(0)
        give_plane(1)
        give_line(0)
        keep(1)
        give_plane(3)
        give_line(1)
        give_plane(0)

        for g, (_, (_, got_t), (msg, got)) in enumerate(groups):
            mine = (mine_p, mine_l)[g]
            got[0] = msg[...]
            wait_for(got.at[pl.ds(1, 15)], small_r.at[2, g])
            share = jnp.exp2(got_t[...] - lse_t[g][None])
            loss = jnp.sum(got[...] * share, axis=0) - lse_t[g] + lse_s[g]
            picked = lax.broadcasted_iota(jnp.int32, loss.shape, 0) == lax.div(mine, 4)
            row = jnp.sum(jnp.where(picked, loss, 0.0), axis=0, keepdims=True)
            turned = pltpu.roll(jnp.broadcast_to(row, (8, 128)), lax.rem(128 - lax.rem(mine, 4) * ROWS, 128), 1)
            (row_out, col_out)[g][...] = turned

        ri[0] = ip[mine_p]
        rt[0] = tc[me.z]
        wait_for(ri.at[pl.ds(1, PLANE - 1)], grad_r.at[0])
        image_out[...] = jnp.sum(ri[...].astype(F32), axis=0)
        wait_for(rt.at[pl.ds(1, Z - 1)], grad_r.at[1])
        text_out[...] = jnp.sum(rt[...].astype(F32), axis=0)
        for n in range(2):
            wait_for(tsib.at[pl.ds(0, cut)], sib_s.at[n])
        wait_for(ri.at[pl.ds(1, PLANE - 1)], grad_s.at[0])
        wait_for(rt.at[pl.ds(1, Z - 1)], grad_s.at[1])

    if stage == 1:
        student_in.other_finish()
        teacher_in.other_finish()
    if stage >= 3:
        for g in range(2):
            for n in range(3):
                wait_for(groups[g][n][1].at[pl.ds(1, 15)], small_s.at[n, g])
            if stage == 3:
                wait_for(groups[g][2][1].at[pl.ds(1, 15)], small_r.at[2, g])
    student_in.end()
    teacher_in.end()


def body(teacher_image, teacher_text, student_image, student_text, stage=4):
    teacher, student = teacher_text.shape[1], student_text.shape[1]
    texts, images = LINE * ROWS, PLANE * ROWS
    chunks = texts // CHUNK
    vmem = pltpu.VMEM
    dma = pltpu.SemaphoreType.DMA
    tile = vmem((texts, images), F32)
    grads = vmem((Z, ROWS, student), BF16)
    args = (teacher_image, teacher_text, student_image, student_text)
    image_sum, text_sum, row, col = pl.pallas_call(
        functools.partial(kernel, stage),
        out_shape=(
            jax.ShapeDtypeStruct((ROWS, student), F32),
            jax.ShapeDtypeStruct((ROWS, student), F32),
            jax.ShapeDtypeStruct((8, 128), F32),
            jax.ShapeDtypeStruct((8, 128), F32),
        ),
        in_specs=[pl.BlockSpec(memory_space=pltpu.HBM)] * 4,
        out_specs=(pl.BlockSpec(memory_space=pltpu.VMEM),) * 4,
        scratch_shapes=[
            vmem((LINE, ROWS, teacher), BF16),
            vmem((LINE, ROWS, student), BF16),
            vmem((PLANE,) + teacher_image.shape, BF16),
            vmem((PLANE,) + student_image.shape, BF16),
            tile,
            tile,
            tile,
            tile,
            tile,
            tile,
            vmem((texts, images), BF16),
            vmem((2, texts, 1), F32),
            vmem((texts, 1), F32),
            vmem((2, chunks, images), F32),
            vmem((2, chunks, images), F32),
            *[vmem((4, 128), F32)] * 6,
            *[vmem((16, 4, 128), F32)] * 6,
            vmem((4, 128), F32),
            vmem((Z, ROWS, student), F32),
            grads,
            grads,
            grads,
            vmem((PLANE, ROWS, student), BF16),
            vmem((ROWS, student), BF16),
            grads,
            vmem((PLANE, ROWS, student), BF16),
            dma((4,)),
            dma((2, 2)),
            dma((2, 9)),
            dma((2, 7)),
            dma((2,)),
            dma((3, 2)),
            dma((3, 2)),
            dma((2,)),
            dma((2,)),
            dma((2,)),
            dma((2,)),
        ],
        compiler_params=pltpu.CompilerParams(
            collective_id=0, has_side_effects=True, vmem_limit_bytes=40 * 1024 * 1024
        ),
        name="distill",
    )(*[pltpu.with_memory_space_constraint(a, pltpu.HBM) for a in args])
    scale = 1.0 / math.sqrt(student)
    log2 = math.log(2.0)
    return (image_sum * scale, text_sum * scale, row[0, :ROWS] * log2, col[0, :ROWS] * log2)


def solution(mesh):
    in_specs = (P("grp", "blk"), P(("blk", "grp"), None), P("grp", "blk"), P(("blk", "grp"), None))
    out_specs = (
        P(("blk", "grp"), None),
        P(("blk", "grp"), None),
        P(("blk", "grp")),
        P(("blk", "grp")),
    )
    return jax.shard_map(body, mesh=mesh, in_specs=in_specs, out_specs=out_specs, check_vma=False)
```
